32 devices in a mesh: tm: 2 (over x), azim: 16 (over z, y, core).
Axes of the slice: x: 2, y: 2, z: 4, core: 2. Of those that a mesh axis runs over, the one named last changes fastest.
Arguments:
- pressure: bfloat16 [256, 160, 256], P('azim', None, 'tm'), may hold values from -6 to 6
Outputs:
- gram_xx: float32 [128, 2, 256, 256], P('azim', None, 'tm')
- gram_xy: float32 [128, 2, 256, 256], P('azim', None, 'tm')
The draws below stay inside these ranges and needn't reach their ends.
All inputs are finite; a program needn't handle non-finite values.
Results may differ from the reference program's by a relative error of at most 0.0046.
Values may be sent and summed in bfloat16 or wider, within the bound.
A program may use at most 64 MiB of HBM per device.

```python
import jax
import jax.numpy as jnp
from jax import lax

THETA = 256
MODES = 128
ROWS = 160
SNAP_DEV = 128
SNAP = 256


def shard_levels(stream_key, extent, cuts, smallest, top_value):
    def one(axis_at, parts):
        heights = jax.random.uniform(jax.random.fold_in(jax.random.fold_in(stream_key, 6), axis_at), (parts,), jnp.float32, smallest / len(cuts), top_value / len(cuts))
        return jnp.repeat(jnp.exp(heights), extent[axis_at] // parts).reshape((-1,) + (1,) * (len(extent) - axis_at - 1))

    loudness = one(*cuts[0])
    for cut in cuts[1:]:
        loudness = loudness * one(*cut)
    return loudness


def normal_values(own_key, extent, width, reach, cuts=(), kind=jnp.bfloat16):
    values = jax.random.normal(own_key, extent, jnp.float32) * width
    if len(cuts) > 0:
        values = shard_levels(own_key, extent, cuts, -0.22, 0.18) * values
    return jnp.clip(values, min=-reach, max=reach).astype(kind)


def setup_inputs(seed: int = 0) -> dict:
    key_list = jax.random.split(jax.random.key(seed), 2)
    pressure = normal_values(key_list[0], (THETA, ROWS, SNAP), 1.0, 6.0, ((0, 16), (2, 2)))
    return dict(pressure=pressure)


def tables():
    angle_idx = jnp.arange(THETA, dtype=jnp.int32)[:, None]
    wave_idx = jnp.arange(MODES, dtype=jnp.int32)[None, :]
    phase = ((angle_idx * wave_idx) % THETA).astype(jnp.float32) * (2.0 * jnp.pi / THETA)
    scale = THETA ** -0.5
    return (jnp.cos(phase) * scale).astype(jnp.bfloat16), (-jnp.sin(phase) * scale).astype(jnp.bfloat16)


def reference(pressure):
    table_cos, table_sin = tables()
    field = pressure.astype(jnp.float32)
    real_part = jnp.einsum("art,am->mrt", field, table_cos.astype(jnp.float32)).astype(jnp.bfloat16)
    imag_part = jnp.einsum("art,am->mrt", field, table_sin.astype(jnp.float32)).astype(jnp.bfloat16)
    modes = jnp.stack([real_part, imag_part], axis=1)
    shifted = jnp.concatenate([modes[..., 1:], jnp.zeros(modes.shape[:3] + (1,), jnp.bfloat16)], axis=3)
    gain = ROWS ** -0.5
    rows_blk = jnp.arange(SNAP, dtype=jnp.int32)[:, None] // SNAP_DEV
    cols_blk = jnp.arange(SNAP, dtype=jnp.int32)[None, :] // SNAP_DEV
    keep = cols_blk <= rows_blk

    def gram(left, right):
        left = left.astype(jnp.float32)
        right = right.astype(jnp.float32)
        real = jnp.dot(left[0].T, right[0], preferred_element_type=jnp.float32) + jnp.dot(left[1].T, right[1], preferred_element_type=jnp.float32)
        imag = jnp.dot(left[0].T, right[1], preferred_element_type=jnp.float32) - jnp.dot(left[1].T, right[0], preferred_element_type=jnp.float32)
        both = jnp.stack([real, imag]) * gain
        return jnp.where(keep[None], both, jnp.float32(0.0))

    def per_mode(items):
        left, right = items
        return gram(left, left), gram(left, right)

    gram_xx, gram_xy = lax.map(per_mode, (modes, shifted))
    return gram_xx, gram_xy
```

```python
import functools

import jax
import jax.numpy as jnp
import ml_dtypes
import numpy as np
from jax import lax
from jax.experimental import pallas as pl
from jax.experimental.pallas import tpu as pltpu
from jax.sharding import PartitionSpec as P

MESH = pl.DeviceIdType.MESH
TILE = 16


def dft_table(theta, parts, group):
    angles = theta // parts
    per_set = theta // 2 // parts
    column = np.arange(theta)
    owner, within = column // (2 * per_set), column % (2 * per_set)
    wave = owner * per_set + within % per_set
    index = (wave[:, None] * np.arange(theta)[None, :]) % theta
    phase = index.astype(np.float32) * np.float32(2.0 * np.pi / theta)
    scale = np.float32(theta ** -0.5)
    imag = (within // per_set == 1)[:, None]
    values = np.where(imag, -np.sin(phase), np.cos(phase)) * scale
    values = values.reshape(parts, 1, 2 * per_set, parts, 1, angles)
    eye = np.eye(group, dtype=np.float32).reshape(1, group, 1, 1, group, 1)
    side = theta * group
    return (values * eye).reshape(side, side).astype(ml_dtypes.bfloat16)


def swap_table(outer, inner):
    row = np.arange(outer * inner)
    source = (row % inner) * outer + row // inner
    return (source[:, None] == row[None, :]).astype(ml_dtypes.bfloat16)


def matmul(a, b):
    return jnp.dot(a, b, preferred_element_type=jnp.float32).astype(jnp.bfloat16)


def exchange_kernel(
    parts, blocks, unit, groups, chunks,
    x_ref, swap_in, swap_out, table, modes_ref,
    pack, rx1, tx, rx2, send1, recv1, send2, recv2, send3, recv3,
):
    me = lax.axis_index("azim")
    tm = lax.axis_index("tm")
    angles, rows, width = x_ref.shape
    blk = unit * groups
    cb = blk // chunks
    per_chunk = groups // chunks
    padded = parts * blk // angles

    barrier = pltpu.get_barrier_semaphore()

    def greet(s, carry):
        pl.semaphore_signal(
            barrier, inc=1, device_id=(tm, lax.rem(me + s, parts)), device_id_type=MESH
        )
        return carry

    lax.fori_loop(1, parts, greet, 0)
    for d in range(1, blocks):
        pl.semaphore_signal(
            barrier, inc=1, device_id=(lax.rem(tm + d, blocks), me), device_id_type=MESH
        )

    step = TILE * angles
    for k in range(padded // TILE):
        if k * TILE < rows:
            part = x_ref[:, k * TILE:(k + 1) * TILE, :].reshape(step, width)
            pack[k * step:(k + 1) * step, :] = matmul(swap_in[...], part)
        else:
            pack[k * step:(k + 1) * step, :] = jnp.zeros((step, width), jnp.bfloat16)

    pl.semaphore_wait(barrier, parts - 1 + blocks - 1)

    def shift(i):
        return 1 + lax.rem(parts // 2 - 1 + i, parts - 1)

    def copy1(c, s):
        to = lax.rem(me + s, parts)
        return pltpu.make_async_remote_copy(
            src_ref=pack.at[pl.ds(pl.multiple_of(to * blk + c * cb, TILE), cb), :],
            dst_ref=rx1.at[me, pl.ds(c * cb, cb), :],
            send_sem=send1.at[c, s],
            recv_sem=recv1.at[c, s],
            device_id=(tm, to),
            device_id_type=MESH,
        )

    def copy2(c, s):
        to = lax.rem(me + s, parts)
        return pltpu.make_async_remote_copy(
            src_ref=tx.at[to, pl.ds(c * cb, cb), :],
            dst_ref=rx2.at[tm, me, pl.ds(c * cb, cb), :],
            send_sem=send2.at[c, s],
            recv_sem=recv2.at[c, s],
            device_id=(tm, to),
            device_id_type=MESH,
        )

    def landed1(c, s):
        source = lax.rem(me + parts - s, parts)
        here = rx1.at[source, pl.ds(c * cb, cb), :]
        return pltpu.make_async_remote_copy(
            src_ref=here, dst_ref=here, send_sem=send1.at[c, s], recv_sem=recv1.at[c, s],
            device_id=(tm, source), device_id_type=MESH,
        )

    def landed2(c, s):
        source = lax.rem(me + parts - s, parts)
        here = rx2.at[tm, source, pl.ds(c * cb, cb), :]
        return pltpu.make_async_remote_copy(
            src_ref=here, dst_ref=here, send_sem=send2.at[c, s], recv_sem=recv2.at[c, s],
            device_id=(tm, source), device_id_type=MESH,
        )

    def copy3(c, source, d):
        here = rx2.at[tm, source, pl.ds(c * cb, cb), :]
        return pltpu.make_async_remote_copy(
            src_ref=here, dst_ref=here,
            send_sem=send3.at[d, c, source], recv_sem=recv3.at[d, c, source],
            device_id=(lax.rem(tm + d, blocks), me), device_id_type=MESH,
        )

    def landed3(c, source, d):
        here = rx2.at[lax.rem(tm + blocks - d, blocks), source, pl.ds(c * cb, cb), :]
        return pltpu.make_async_remote_copy(
            src_ref=here, dst_ref=here,
            send_sem=send3.at[d, c, source], recv_sem=recv3.at[d, c, source],
            device_id=(lax.rem(tm + blocks - d, blocks), me), device_id_type=MESH,
        )

    def guarded(condition, act):
        if blocks == 2:
            act()
        else:
            pl.when(condition)(act)

    def needed_by(d):
        return lax.rem(tm + d, blocks) >= tm - 1

    def needed_from(d):
        return lax.rem(tm + blocks - d, blocks) <= tm + 1

    def loop(body):
        def run(i, carry):
            body(shift(i))
            return carry
        lax.fori_loop(0, parts - 1, run, 0)

    def forward(c, source):
        for d in range(1, blocks):
            guarded(needed_by(d), lambda d=d: copy3(c, source, d).start())

    for c in range(chunks):
        loop(lambda s, c=c: copy1(c, s).start())
    rx1[pl.ds(me, 1)] = pack[pl.ds(pl.multiple_of(me * blk, TILE), blk), :].reshape(1, blk, width)

    for c in range(chunks):
        loop(lambda s, c=c: landed1(c, s).wait_recv())
        for q in range(c * per_chunk, (c + 1) * per_chunk):
            field = rx1[:, q * unit:(q + 1) * unit, :].reshape(parts * unit, width)
            tx[:, q * unit:(q + 1) * unit, :] = matmul(table[...], field).reshape(parts, unit, width)
        loop(lambda s, c=c: copy2(c, s).start())
        rx2[tm, me, c * cb:(c + 1) * cb, :] = tx[me, c * cb:(c + 1) * cb, :]
        forward(c, me)

    for c in range(chunks):
        def pass_on(s, c=c):
            landed2(c, s).wait_recv()
            forward(c, lax.rem(me + parts - s, parts))
        loop(pass_on)

    def regroup(block):
        step_out = TILE * angles
        flat = rx2.at[block].reshape(parts * blk, width)
        for k in range(padded // TILE):
            tile = matmul(swap_out[...], flat[k * step_out:(k + 1) * step_out, :])
            modes_ref[:, k * TILE:(k + 1) * TILE, pl.ds(pl.multiple_of(block * width, width), width)] = (
                tile.reshape(angles, TILE, width)
            )

    regroup(tm)
    for d in range(1, blocks):
        def take(d=d):
            for c in range(chunks):
                def arrive(i, carry, c=c):
                    landed3(c, lax.rem(me + i, parts), d).wait_recv()
                    return carry
                lax.fori_loop(0, parts, arrive, 0)
            regroup(lax.rem(tm + blocks - d, blocks))

        guarded(needed_from(d), take)
        if blocks > 2:
            @pl.when(jnp.logical_not(needed_from(d)))
            def _(d=d):
                other = lax.rem(tm + blocks - d, blocks)
                modes_ref[:, :, pl.ds(pl.multiple_of(other * width, width), width)] = jnp.zeros(
                    (angles, padded, width), jnp.bfloat16
                )

    for c in range(chunks):
        loop(lambda s, c=c: copy1(c, s).wait_send())
        loop(lambda s, c=c: copy2(c, s).wait_send())
        for d in range(1, blocks):
            def sent(d=d, c=c):
                def one(i, carry):
                    copy3(c, i, d).wait_send()
                    return carry
                lax.fori_loop(0, parts, one, 0)
            guarded(needed_by(d), sent)


def gram_kernel(gain, width, modes_ref, xx_ref, xy_ref):
    tm = lax.axis_index("tm")
    count, full = modes_ref.shape[1], modes_ref.shape[3]
    limit = (tm + 1) * width
    columns = lax.broadcasted_iota(jnp.int32, (width, full), 1)
    keep_xx = columns < limit
    keep_xy = columns < jnp.minimum(limit, full - 1)
    own = pl.ds(pl.multiple_of(tm * width, width), width)
    for m in range(count):
        real, imag = modes_ref[0, m], modes_ref[1, m]
        left = jnp.concatenate([modes_ref[0, m, :, own], modes_ref[1, m, :, own]], axis=0)
        for p, right in ((0, [real, imag]), (1, [imag, -real])):
            product = lax.dot_general(
                left, jnp.concatenate(right, axis=0), (((0,), (0,)), ((), ())),
                preferred_element_type=jnp.float32,
            ) * gain
            xx_ref[m, p] = jnp.where(keep_xx, product, 0.0)
            xy_ref[m, p] = jnp.where(keep_xy, pltpu.roll(product, full - 1, 1), 0.0)


def body(parts, blocks, pressure):
    angles, rows, width = pressure.shape
    theta = angles * parts
    per_set = theta // 2 // parts
    group = max(1, TILE // angles)
    unit = group * angles
    groups = -(-rows // (parts * group))
    while parts * groups * group % TILE:
        groups += 1
    chunks = 2 if groups % 2 == 0 else 1
    blk = unit * groups
    padded = parts * groups * group
    full = blocks * width

    vmem = pl.BlockSpec(memory_space=pltpu.VMEM)
    dma = pltpu.SemaphoreType.DMA
    modes = pl.pallas_call(
        functools.partial(exchange_kernel, parts, blocks, unit, groups, chunks),
        out_shape=jax.ShapeDtypeStruct((angles, padded, full), jnp.bfloat16),
        in_specs=[vmem] * 4,
        out_specs=vmem,
        scratch_shapes=[
            pltpu.VMEM((parts * blk, width), jnp.bfloat16),
            pltpu.VMEM((parts, blk, width), jnp.bfloat16),
            pltpu.VMEM((parts, blk, width), jnp.bfloat16),
            pltpu.VMEM((blocks, parts, blk, width), jnp.bfloat16),
            dma((chunks, parts)), dma((chunks, parts)),
            dma((chunks, parts)), dma((chunks, parts)),
            dma((blocks, chunks, parts)), dma((blocks, chunks, parts)),
        ],
        compiler_params=pltpu.CompilerParams(
            collective_id=0, has_side_effects=True, vmem_limit_bytes=48 * 2**20
        ),
        name="exchange",
    )(
        pressure,
        jnp.asarray(swap_table(TILE, angles)),
        jnp.asarray(swap_table(angles, TILE)),
        jnp.asarray(dft_table(theta, parts, group)),
    )
    modes = modes.reshape(2, per_set, padded, full)
    shape = jax.ShapeDtypeStruct((per_set, 2, width, full), jnp.float32)
    out = pl.BlockSpec((1, 2, width, full), lambda i: (i, 0, 0, 0))
    return pl.pallas_call(
        functools.partial(gram_kernel, rows ** -0.5, width),
        grid=(per_set,),
        out_shape=(shape, shape),
        in_specs=[pl.BlockSpec((2, 1, padded, full), lambda i: (0, i, 0, 0))],
        out_specs=(out, out),
        compiler_params=pltpu.CompilerParams(vmem_limit_bytes=48 * 2**20),
        name="grams",
    )(modes)


def solution(mesh):
    parts, blocks = mesh.shape["azim"], mesh.shape["tm"]
    in_specs = (P("azim", None, "tm"),)
    out_specs = (P("azim", None, "tm", None), P("azim", None, "tm", None))
    return jax.shard_map(
        functools.partial(body, parts, blocks),
        mesh=mesh, in_specs=in_specs, out_specs=out_specs, check_vma=False,
    )
```

```python
import functools

import jax
import jax.numpy as jnp
import ml_dtypes
import numpy as np
from jax import lax
from jax.experimental import pallas as pl
from jax.experimental.pallas import tpu as pltpu
from jax.sharding import PartitionSpec as P

MESH = pl.DeviceIdType.MESH
TILE = 16


def dft_table(theta, parts, group):
    angles = theta // parts
    per_set = theta // 2 // parts
    column = np.arange(theta)
    owner, within = column // (2 * per_set), column % (2 * per_set)
    wave = owner * per_set + within % per_set
    index = (wave[:, None] * np.arange(theta)[None, :]) % theta
    phase = index.astype(np.float32) * np.float32(2.0 * np.pi / theta)
    scale = np.float32(theta ** -0.5)
    imag = (within // per_set == 1)[:, None]
    values = np.where(imag, -np.sin(phase), np.cos(phase)) * scale
    values = values.reshape(parts, 1, 2 * per_set, parts, 1, angles)
    eye = np.eye(group, dtype=np.float32).reshape(1, group, 1, 1, group, 1)
    side = theta * group
    return (values * eye).reshape(side, side).astype(ml_dtypes.bfloat16)


def swap_table(outer, inner):
    row = np.arange(outer * inner)
    source = (row % inner) * outer + row // inner
    return (source[:, None] == row[None, :]).astype(ml_dtypes.bfloat16)


def matmul(a, b):
    return jnp.dot(a, b, preferred_element_type=jnp.float32).astype(jnp.bfloat16)


def exchange_kernel(
    parts, blocks, unit, groups, chunks,
    x_hbm, swap_in_hbm, swap_out_hbm, table_hbm, modes_ref,
    x_ref, swap_in, swap_out, table, pack, rx1, tx, rx2,
    load, send1, recv1, send2, recv2, send3, recv3,
):
    me = lax.axis_index("azim")
    tm = lax.axis_index("tm")
    angles, rows, width = x_ref.shape
    blk = unit * groups
    cb = blk // chunks
    per_chunk = groups // chunks
    padded = parts * blk // angles

    loads = [
        pltpu.make_async_copy(src, dst, load.at[i])
        for i, (src, dst) in enumerate(
            ((swap_in_hbm, swap_in), (x_hbm, x_ref), (table_hbm, table), (swap_out_hbm, swap_out))
        )
    ]
    for copy in loads:
        copy.start()

    barrier = pltpu.get_barrier_semaphore()

    def peer(s):
        other, bit = 0, 1
        while bit < parts:
            mine, flip = lax.rem(me // bit, 2), lax.rem(s // bit, 2)
            other = other + bit * (mine + flip - 2 * mine * flip)
            bit *= 2
        return other

    def greet(s, carry):
        pl.semaphore_signal(barrier, inc=1, device_id=(tm, peer(s)), device_id_type=MESH)
        return carry

    lax.fori_loop(1, parts, greet, 0)
    for d in range(1, blocks):
        pl.semaphore_signal(
            barrier, inc=1, device_id=(lax.rem(tm + d, blocks), me), device_id_type=MESH
        )

    loads[0].wait()
    loads[1].wait()
    step = TILE * angles
    for k in range(padded // TILE):
        if k * TILE < rows:
            part = x_ref[:, k * TILE:(k + 1) * TILE, :].reshape(step, width)
            pack[k * step:(k + 1) * step, :] = matmul(swap_in[...], part)
        else:
            pack[k * step:(k + 1) * step, :] = jnp.zeros((step, width), jnp.bfloat16)

    pl.semaphore_wait(barrier, parts - 1 + blocks - 1)

    def shift(i):
        odd = lax.rem(i, 2)
        return i // 2 + odd + (parts // 2) * (1 - odd)

    def copy1(c, s):
        to = peer(s)
        return pltpu.make_async_remote_copy(
            src_ref=pack.at[pl.ds(pl.multiple_of(to * blk + c * cb, TILE), cb), :],
            dst_ref=rx1.at[c, me],
            send_sem=send1.at[c, s],
            recv_sem=recv1.at[c, s],
            device_id=(tm, to),
            device_id_type=MESH,
        )

    def copy2(c, s):
        to = peer(s)
        return pltpu.make_async_remote_copy(
            src_ref=tx.at[c, to],
            dst_ref=rx2.at[tm, c, me],
            send_sem=send2.at[c, s],
            recv_sem=recv2.at[c, s],
            device_id=(tm, to),
            device_id_type=MESH,
        )

    def landed1(c, s):
        source = peer(s)
        here = rx1.at[c, source]
        return pltpu.make_async_remote_copy(
            src_ref=here, dst_ref=here, send_sem=send1.at[c, s], recv_sem=recv1.at[c, s],
            device_id=(tm, source), device_id_type=MESH,
        )

    def landed2(c, s):
        source = peer(s)
        here = rx2.at[tm, c, source]
        return pltpu.make_async_remote_copy(
            src_ref=here, dst_ref=here, send_sem=send2.at[c, s], recv_sem=recv2.at[c, s],
            device_id=(tm, source), device_id_type=MESH,
        )

    def copy3(c, source, d):
        here = rx2.at[tm, c, source]
        return pltpu.make_async_remote_copy(
            src_ref=here, dst_ref=here,
            send_sem=send3.at[d, c, source], recv_sem=recv3.at[d, c, source],
            device_id=(lax.rem(tm + d, blocks), me), device_id_type=MESH,
        )

    def landed3(c, source, d):
        here = rx2.at[lax.rem(tm + blocks - d, blocks), c, source]
        return pltpu.make_async_remote_copy(
            src_ref=here, dst_ref=here,
            send_sem=send3.at[d, c, source], recv_sem=recv3.at[d, c, source],
            device_id=(lax.rem(tm + blocks - d, blocks), me), device_id_type=MESH,
        )

    def guarded(condition, act):
        if blocks == 2:
            act()
        else:
            pl.when(condition)(act)

    def needed_by(d):
        return lax.rem(tm + d, blocks) >= tm - 1

    def needed_from(d):
        return lax.rem(tm + blocks - d, blocks) <= tm + 1

    def loop(body):
        def run(i, carry):
            body(shift(i))
            return carry
        lax.fori_loop(0, parts - 1, run, 0)

    def forward(c, source):
        for d in range(1, blocks):
            guarded(needed_by(d), lambda d=d: copy3(c, source, d).start())

    for c in range(chunks):
        loop(lambda s, c=c: copy1(c, s).start())
        rx1[c, me] = pack[pl.ds(pl.multiple_of(me * blk + c * cb, TILE), cb), :]
    loads[2].wait()
    loads[3].wait()

    for c in range(chunks):
        loop(lambda s, c=c: landed1(c, s).wait_recv())
        for q in range(per_chunk):
            field = rx1[c, :, q * unit:(q + 1) * unit, :].reshape(parts * unit, width)
            tx[c, :, q * unit:(q + 1) * unit, :] = matmul(table[...], field).reshape(parts, unit, width)
        loop(lambda s, c=c: copy2(c, s).start())
        rx2[tm, c, me] = tx[c, me]
        forward(c, me)

    span = padded // chunks

    def regroup(block, c):
        for k in range(span // TILE):
            rows_in = rx2.at[block, c].reshape(parts * cb, width)[k * step:(k + 1) * step, :]
            modes_ref[
                :, c * span + k * TILE:c * span + (k + 1) * TILE,
                pl.ds(pl.multiple_of(block * width, width), width),
            ] = matmul(swap_out[...], rows_in).reshape(angles, TILE, width)

    for c in range(chunks):
        def pass_on(s, c=c):
            landed2(c, s).wait_recv()
            forward(c, peer(s))
        loop(pass_on)
        regroup(tm, c)

    for d in range(1, blocks):
        def take(d=d):
            for c in range(chunks):
                def arrive(i, carry, c=c):
                    landed3(c, i, d).wait_recv()
                    return carry
                lax.fori_loop(0, parts, arrive, 0)
                regroup(lax.rem(tm + blocks - d, blocks), c)

        guarded(needed_from(d), take)
        if blocks > 2:
            @pl.when(jnp.logical_not(needed_from(d)))
            def _(d=d):
                other = lax.rem(tm + blocks - d, blocks)
                modes_ref[:, :, pl.ds(pl.multiple_of(other * width, width), width)] = jnp.zeros(
                    (angles, padded, width), jnp.bfloat16
                )

    for c in range(chunks):
        loop(lambda s, c=c: copy1(c, s).wait_send())
        loop(lambda s, c=c: copy2(c, s).wait_send())
        for d in range(1, blocks):
            def sent(d=d, c=c):
                def one(i, carry):
                    copy3(c, i, d).wait_send()
                    return carry
                lax.fori_loop(0, parts, one, 0)
            guarded(needed_by(d), sent)


def gram_kernel(gain, width, modes_ref, xx_ref, xy_ref):
    tm = lax.axis_index("tm")
    count, full = modes_ref.shape[1], modes_ref.shape[3]
    limit = (tm + 1) * width
    columns = lax.broadcasted_iota(jnp.int32, (width, full), 1)
    keep_xx = columns < limit
    keep_xy = columns < jnp.minimum(limit, full - 1)
    own = pl.ds(pl.multiple_of(tm * width, width), width)
    for m in range(count):
        real, imag = modes_ref[0, m], modes_ref[1, m]
        left = jnp.concatenate([modes_ref[0, m, :, own], modes_ref[1, m, :, own]], axis=0)
        for p, right in ((0, [real, imag]), (1, [imag, -real])):
            product = lax.dot_general(
                left, jnp.concatenate(right, axis=0), (((0,), (0,)), ((), ())),
                preferred_element_type=jnp.float32,
            ) * gain
            xx_ref[m, p] = jnp.where(keep_xx, product, 0.0)
            xy_ref[m, p] = jnp.where(keep_xy, pltpu.roll(product, full - 1, 1), 0.0)


def body(parts, blocks, pressure):
    angles, rows, width = pressure.shape
    theta = angles * parts
    per_set = theta // 2 // parts
    group = max(1, TILE // angles)
    unit = group * angles
    groups = -(-rows // (parts * group))
    while parts * groups * group % TILE:
        groups += 1
    blk = unit * groups
    padded = parts * groups * group
    chunks = 2 if groups % 2 == 0 and padded % (2 * TILE) == 0 else 1
    full = blocks * width

    swap = swap_table(TILE, angles)
    table = dft_table(theta, parts, group)
    vmem = pl.BlockSpec(memory_space=pltpu.VMEM)
    dma = pltpu.SemaphoreType.DMA
    modes = pl.pallas_call(
        functools.partial(exchange_kernel, parts, blocks, unit, groups, chunks),
        out_shape=jax.ShapeDtypeStruct((angles, padded, full), jnp.bfloat16),
        in_specs=[pl.BlockSpec(memory_space=pltpu.HBM)] * 4,
        out_specs=vmem,
        scratch_shapes=[
            pltpu.VMEM(pressure.shape, jnp.bfloat16),
            pltpu.VMEM(swap.shape, jnp.bfloat16),
            pltpu.VMEM(swap.shape, jnp.bfloat16),
            pltpu.VMEM(table.shape, jnp.bfloat16),
            pltpu.VMEM((parts * blk, width), jnp.bfloat16),
            pltpu.VMEM((chunks, parts, blk // chunks, width), jnp.bfloat16),
            pltpu.VMEM((chunks, parts, blk // chunks, width), jnp.bfloat16),
            pltpu.VMEM((blocks, chunks, parts, blk // chunks, width), jnp.bfloat16),
            dma((4,)),
            dma((chunks, parts)), dma((chunks, parts)),
            dma((chunks, parts)), dma((chunks, parts)),
            dma((blocks, chunks, parts)), dma((blocks, chunks, parts)),
        ],
        compiler_params=pltpu.CompilerParams(
            collective_id=0, has_side_effects=True, vmem_limit_bytes=48 * 2**20
        ),
        name="exchange",
    )(
        pressure,
        jnp.asarray(swap),
        jnp.asarray(swap_table(angles, TILE)),
        jnp.asarray(table),
    )
    modes = modes.reshape(2, per_set, padded, full)
    shape = jax.ShapeDtypeStruct((per_set, 2, width, full), jnp.float32)
    out = pl.BlockSpec((1, 2, width, full), lambda i: (i, 0, 0, 0))
    return pl.pallas_call(
        functools.partial(gram_kernel, rows ** -0.5, width),
        grid=(per_set,),
        out_shape=(shape, shape),
        in_specs=[pl.BlockSpec((2, 1, padded, full), lambda i: (0, i, 0, 0))],
        out_specs=(out, out),
        compiler_params=pltpu.CompilerParams(vmem_limit_bytes=48 * 2**20),
        name="grams",
    )(modes)


def solution(mesh):
    parts, blocks = mesh.shape["azim"], mesh.shape["tm"]
    in_specs = (P("azim", None, "tm"),)
    out_specs = (P("azim", None, "tm", None), P("azim", None, "tm", None))
    return jax.shard_map(
        functools.partial(body, parts, blocks),
        mesh=mesh, in_specs=in_specs, out_specs=out_specs, check_vma=False,
    )
```

```python
import functools

import jax
import jax.numpy as jnp
import numpy as np
from jax import lax
from jax.experimental import pallas as pl
from jax.experimental.pallas import tpu as pltpu
from jax.sharding import PartitionSpec as P

MESH = pl.DeviceIdType.MESH
TILE = 16


def dft_table(theta, parts, group):
    angles = theta // parts
    per_set = angles // 2
    side = theta * group
    row = lax.broadcasted_iota(jnp.int32, (side, side), 0)
    column = lax.broadcasted_iota(jnp.int32, (side, side), 1)
    unit = angles * group
    within = row & (angles - 1)
    imag = (within >= per_set).astype(jnp.int32)
    wave = (row // unit) * per_set + (within & (per_set - 1))
    angle = (column // unit) * angles + (column & (angles - 1))
    index = (wave * angle + imag * (theta // 4)) & (theta - 1)
    index = jnp.where(index >= theta // 2, index - theta, index)
    values = jnp.cos(index.astype(jnp.float32) * (2.0 * np.pi / theta)) * theta ** -0.5
    if group > 1:
        same = (row & (unit - 1)) // angles == (column & (unit - 1)) // angles
        values = jnp.where(same, values, 0.0)
    return values.astype(jnp.bfloat16)


def swap_table(outer, inner):
    row = lax.broadcasted_iota(jnp.int32, (outer * inner, outer * inner), 0)
    column = lax.broadcasted_iota(jnp.int32, (outer * inner, outer * inner), 1)
    hit = (row & (inner - 1)) * outer + row // inner == column
    return jnp.where(hit, 1.0, 0.0).astype(jnp.bfloat16)


def matmul(a, b):
    return jnp.dot(a, b, preferred_element_type=jnp.float32).astype(jnp.bfloat16)


def exchange_kernel(
    parts, blocks, unit, groups, chunks,
    x_ref, modes_ref,
    swap_in, swap_out, table, pack, rx1, tx, rx2,
    send1, recv1, send2, recv2, send3, recv3,
):
    me = lax.axis_index("azim")
    tm = lax.axis_index("tm")
    angles, rows, width = x_ref.shape
    blk = unit * groups
    cb = blk // chunks
    per_chunk = groups // chunks
    padded = parts * blk // angles

    barrier = pltpu.get_barrier_semaphore()

    def peer(s):
        other, bit = 0, 1
        while bit < parts:
            mine, flip = lax.rem(me // bit, 2), lax.rem(s // bit, 2)
            other = other + bit * (mine + flip - 2 * mine * flip)
            bit *= 2
        return other

    def greet(s, carry):
        pl.semaphore_signal(barrier, inc=1, device_id=(tm, peer(s)), device_id_type=MESH)
        return carry

    lax.fori_loop(1, parts, greet, 0)
    for d in range(1, blocks):
        pl.semaphore_signal(
            barrier, inc=1, device_id=(lax.rem(tm + d, blocks), me), device_id_type=MESH
        )

    swap_in[...] = swap_table(TILE, angles)
    step = TILE * angles
    for k in range(padded // TILE):
        if k * TILE < rows:
            part = x_ref[:, k * TILE:(k + 1) * TILE, :].reshape(step, width)
            pack[k * step:(k + 1) * step, :] = matmul(swap_in[...], part)
        else:
            pack[k * step:(k + 1) * step, :] = jnp.zeros((step, width), jnp.bfloat16)

    pl.semaphore_wait(barrier, parts - 1 + blocks - 1)

    parity = lax.rem(me, 2)
    half = parts // 2

    def shift(i):
        return 1 + lax.rem((1 - parity) * (half - 1) + i, parts - 1)

    def copy1(c, s):
        to = peer(s)
        return pltpu.make_async_remote_copy(
            src_ref=pack.at[pl.ds(pl.multiple_of(to * blk + c * cb, TILE), cb), :],
            dst_ref=rx1.at[c, me],
            send_sem=send1.at[c, s],
            recv_sem=recv1.at[c, s],
            device_id=(tm, to),
            device_id_type=MESH,
        )

    def copy2(c, s):
        to = peer(s)
        return pltpu.make_async_remote_copy(
            src_ref=tx.at[c, to],
            dst_ref=rx2.at[tm, c, me],
            send_sem=send2.at[c, s],
            recv_sem=recv2.at[c, s],
            device_id=(tm, to),
            device_id_type=MESH,
        )

    def landed1(c, s):
        source = peer(s)
        here = rx1.at[c, source]
        return pltpu.make_async_remote_copy(
            src_ref=here, dst_ref=here, send_sem=send1.at[c, s], recv_sem=recv1.at[c, s],
            device_id=(tm, source), device_id_type=MESH,
        )

    def landed2(c, s):
        source = peer(s)
        here = rx2.at[tm, c, source]
        return pltpu.make_async_remote_copy(
            src_ref=here, dst_ref=here, send_sem=send2.at[c, s], recv_sem=recv2.at[c, s],
            device_id=(tm, source), device_id_type=MESH,
        )

    def copy3(c, source, d):
        here = rx2.at[tm, c, source]
        return pltpu.make_async_remote_copy(
            src_ref=here, dst_ref=here,
            send_sem=send3.at[d, c, source], recv_sem=recv3.at[d, c, source],
            device_id=(lax.rem(tm + d, blocks), me), device_id_type=MESH,
        )

    def landed3(c, source, d):
        here = rx2.at[lax.rem(tm + blocks - d, blocks), c, source]
        return pltpu.make_async_remote_copy(
            src_ref=here, dst_ref=here,
            send_sem=send3.at[d, c, source], recv_sem=recv3.at[d, c, source],
            device_id=(lax.rem(tm + blocks - d, blocks), me), device_id_type=MESH,
        )

    def guarded(condition, act):
        if blocks == 2:
            act()
        else:
            pl.when(condition)(act)

    def needed_by(d):
        return lax.rem(tm + d, blocks) >= tm - 1

    def needed_from(d):
        return lax.rem(tm + blocks - d, blocks) <= tm + 1

    def loop(body):
        def run(i, carry):
            body(shift(i))
            return carry
        lax.fori_loop(0, parts - 1, run, 0)

    def forward(c, source):
        for d in range(1, blocks):
            guarded(needed_by(d), lambda d=d: copy3(c, source, d).start())

    for c in range(chunks):
        loop(lambda s, c=c: copy1(c, s).start())
        rx1[c, me] = pack[pl.ds(pl.multiple_of(me * blk + c * cb, TILE), cb), :]
    swap_out[...] = swap_table(angles, TILE)
    table[...] = dft_table(angles * parts, parts, unit // angles)

    for c in range(chunks):
        loop(lambda s, c=c: landed1(c, s).wait_recv())
        for q in range(per_chunk):
            field = rx1[c, :, q * unit:(q + 1) * unit, :].reshape(parts * unit, width)
            tx[c, :, q * unit:(q + 1) * unit, :] = matmul(table[...], field).reshape(parts, unit, width)
        loop(lambda s, c=c: copy2(c, s).start())
        rx2[tm, c, me] = tx[c, me]
        forward(c, me)

    span = padded // chunks

    def regroup(block, c):
        for k in range(span // TILE):
            rows_in = rx2.at[block, c].reshape(parts * cb, width)[k * step:(k + 1) * step, :]
            modes_ref[
                :, c * span + k * TILE:c * span + (k + 1) * TILE,
                pl.ds(pl.multiple_of(block * width, width), width),
            ] = matmul(swap_out[...], rows_in).reshape(angles, TILE, width)

    for c in range(chunks):
        def pass_on(s, c=c):
            landed2(c, s).wait_recv()
            forward(c, peer(s))

        for late in range(2):
            flag = parity if late == 0 else 1 - parity

            def far(j, carry, flag=flag):
                pass_on(half + 2 * j + flag)
                return carry

            def near(j, carry, flag=flag):
                s = 2 * j + 1 - flag
                pl.when(s > 0)(lambda: pass_on(s))
                return carry

            lax.fori_loop(0, half // 2, near, 0)
            lax.fori_loop(0, half // 2, far, 0)
        regroup(tm, c)

    for d in range(1, blocks):
        def take(d=d):
            for c in range(chunks):
                def arrive(i, carry, c=c):
                    landed3(c, i, d).wait_recv()
                    return carry
                lax.fori_loop(0, parts, arrive, 0)
                regroup(lax.rem(tm + blocks - d, blocks), c)

        guarded(needed_from(d), take)
        if blocks > 2:
            @pl.when(jnp.logical_not(needed_from(d)))
            def _(d=d):
                other = lax.rem(tm + blocks - d, blocks)
                modes_ref[:, :, pl.ds(pl.multiple_of(other * width, width), width)] = jnp.zeros(
                    (angles, padded, width), jnp.bfloat16
                )

    for c in range(chunks):
        loop(lambda s, c=c: copy1(c, s).wait_send())
        loop(lambda s, c=c: copy2(c, s).wait_send())
        for d in range(1, blocks):
            def sent(d=d, c=c):
                def one(i, carry):
                    copy3(c, i, d).wait_send()
                    return carry
                lax.fori_loop(0, parts, one, 0)
            guarded(needed_by(d), sent)


def gram_kernel(gain, width, modes_ref, xx_ref, xy_ref):
    tm = lax.axis_index("tm")
    count, full = modes_ref.shape[1], modes_ref.shape[3]
    limit = (tm + 1) * width
    columns = lax.broadcasted_iota(jnp.int32, (width, full), 1)
    keep_xx = columns < limit
    keep_xy = columns < jnp.minimum(limit, full - 1)
    own = pl.ds(pl.multiple_of(tm * width, width), width)
    for m in range(count):
        real, imag = modes_ref[0, m], modes_ref[1, m]
        left = jnp.concatenate([modes_ref[0, m, :, own], modes_ref[1, m, :, own]], axis=0)
        for p, right in ((0, [real, imag]), (1, [imag, -real])):
            product = lax.dot_general(
                left, jnp.concatenate(right, axis=0), (((0,), (0,)), ((), ())),
                preferred_element_type=jnp.float32,
            ) * gain
            xx_ref[m, p] = jnp.where(keep_xx, product, 0.0)
            xy_ref[m, p] = jnp.where(keep_xy, pltpu.roll(product, full - 1, 1), 0.0)


def body(parts, blocks, pressure):
    angles, rows, width = pressure.shape
    theta = angles * parts
    per_set = theta // 2 // parts
    group = max(1, TILE // angles)
    unit = group * angles
    groups = -(-rows // (parts * group))
    while parts * groups * group % TILE:
        groups += 1
    blk = unit * groups
    padded = parts * groups * group
    chunks = 2 if groups % 2 == 0 and padded % (2 * TILE) == 0 else 1
    full = blocks * width

    vmem = pl.BlockSpec(memory_space=pltpu.VMEM)
    dma = pltpu.SemaphoreType.DMA
    modes = pl.pallas_call(
        functools.partial(exchange_kernel, parts, blocks, unit, groups, chunks),
        out_shape=jax.ShapeDtypeStruct((angles, padded, full), jnp.bfloat16),
        in_specs=[vmem],
        out_specs=vmem,
        scratch_shapes=[
            pltpu.VMEM((TILE * angles, TILE * angles), jnp.bfloat16),
            pltpu.VMEM((TILE * angles, TILE * angles), jnp.bfloat16),
            pltpu.VMEM((theta * group, theta * group), jnp.bfloat16),
            pltpu.VMEM((parts * blk, width), jnp.bfloat16),
            pltpu.VMEM((chunks, parts, blk // chunks, width), jnp.bfloat16),
            pltpu.VMEM((chunks, parts, blk // chunks, width), jnp.bfloat16),
            pltpu.VMEM((blocks, chunks, parts, blk // chunks, width), jnp.bfloat16),
            dma((chunks, parts)), dma((chunks, parts)),
            dma((chunks, parts)), dma((chunks, parts)),
            dma((blocks, chunks, parts)), dma((blocks, chunks, parts)),
        ],
        compiler_params=pltpu.CompilerParams(
            collective_id=0, has_side_effects=True, vmem_limit_bytes=48 * 2**20
        ),
        name="exchange",
    )(pressure)
    modes = modes.reshape(2, per_set, padded, full)
    shape = jax.ShapeDtypeStruct((per_set, 2, width, full), jnp.float32)
    out = pl.BlockSpec((1, 2, width, full), lambda i: (i, 0, 0, 0))
    return pl.pallas_call(
        functools.partial(gram_kernel, rows ** -0.5, width),
        grid=(per_set,),
        out_shape=(shape, shape),
        in_specs=[pl.BlockSpec((2, 1, padded, full), lambda i: (0, i, 0, 0))],
        out_specs=(out, out),
        compiler_params=pltpu.CompilerParams(vmem_limit_bytes=48 * 2**20),
        name="grams",
    )(modes)


def solution(mesh):
    parts, blocks = mesh.shape["azim"], mesh.shape["tm"]
    in_specs = (P("azim", None, "tm"),)
    out_specs = (P("azim", None, "tm", None), P("azim", None, "tm", None))
    return jax.shard_map(
        functools.partial(body, parts, blocks),
        mesh=mesh, in_specs=in_specs, out_specs=out_specs, check_vma=False,
    )
```

```python
import functools

import jax
import jax.numpy as jnp
import numpy as np
from jax import lax
from jax.experimental import pallas as pl
from jax.experimental.pallas import tpu as pltpu
from jax.sharding import PartitionSpec as P

MESH = pl.DeviceIdType.MESH
TILE = 16


def dft_table(theta, parts, group):
    angles = theta // parts
    per_set = angles // 2
    side = theta * group
    row = lax.broadcasted_iota(jnp.int32, (side, side), 0)
    column = lax.broadcasted_iota(jnp.int32, (side, side), 1)
    unit = angles * group
    within = row & (angles - 1)
    imag = (within >= per_set).astype(jnp.int32)
    wave = (row // unit) * per_set + (within & (per_set - 1))
    angle = (column // unit) * angles + (column & (angles - 1))
    index = (wave * angle + imag * (theta // 4)) & (theta - 1)
    index = jnp.where(index >= theta // 2, index - theta, index)
    values = jnp.cos(index.astype(jnp.float32) * (2.0 * np.pi / theta)) * theta ** -0.5
    if group > 1:
        same = (row & (unit - 1)) // angles == (column & (unit - 1)) // angles
        values = jnp.where(same, values, 0.0)
    return values.astype(jnp.bfloat16)


def swap_table(outer, inner):
    row = lax.broadcasted_iota(jnp.int32, (outer * inner, outer * inner), 0)
    column = lax.broadcasted_iota(jnp.int32, (outer * inner, outer * inner), 1)
    hit = (row & (inner - 1)) * outer + row // inner == column
    return jnp.where(hit, 1.0, 0.0).astype(jnp.bfloat16)


def matmul(a, b):
    return jnp.dot(a, b, preferred_element_type=jnp.float32).astype(jnp.bfloat16)


def exchange_kernel(
    parts, blocks, unit, groups, chunks,
    x_ref, modes_ref,
    swap_in, swap_out, table, pack, rx1, tx, rx2,
    send1, recv1, send2, recv2, send3, recv3,
):
    me = lax.axis_index("azim")
    tm = lax.axis_index("tm")
    angles, rows, width = x_ref.shape
    blk = unit * groups
    cb = blk // chunks
    per_chunk = groups // chunks
    padded = parts * blk // angles

    barrier = pltpu.get_barrier_semaphore()

    def peer(s):
        other, bit = 0, 1
        while bit < parts:
            mine, flip = lax.rem(me // bit, 2), lax.rem(s // bit, 2)
            other = other + bit * (mine + flip - 2 * mine * flip)
            bit *= 2
        return other

    def greet(s, carry):
        pl.semaphore_signal(barrier, inc=1, device_id=(tm, peer(s)), device_id_type=MESH)
        return carry

    lax.fori_loop(1, parts, greet, 0)
    for d in range(1, blocks):
        pl.semaphore_signal(
            barrier, inc=1, device_id=(lax.rem(tm + d, blocks), me), device_id_type=MESH
        )

    swap_in[...] = swap_table(TILE, angles)
    step = TILE * angles
    for k in range(padded // TILE):
        if k * TILE < rows:
            part = x_ref[:, k * TILE:(k + 1) * TILE, :].reshape(step, width)
            pack[k * step:(k + 1) * step, :] = matmul(swap_in[...], part)
        else:
            pack[k * step:(k + 1) * step, :] = jnp.zeros((step, width), jnp.bfloat16)

    pl.semaphore_wait(barrier, parts - 1 + blocks - 1)

    parity = lax.rem(me, 2)
    half = parts // 2

    def shift(i):
        return 1 + lax.rem((1 - parity) * (half - 1) + i, parts - 1)

    def copy1(c, s):
        to = peer(s)
        return pltpu.make_async_remote_copy(
            src_ref=pack.at[pl.ds(pl.multiple_of(to * blk + c * cb, TILE), cb), :],
            dst_ref=rx1.at[c, me],
            send_sem=send1.at[c, s],
            recv_sem=recv1.at[c, s],
            device_id=(tm, to),
            device_id_type=MESH,
        )

    def copy2(c, s):
        to = peer(s)
        return pltpu.make_async_remote_copy(
            src_ref=tx.at[c, to],
            dst_ref=rx2.at[tm, c, me],
            send_sem=send2.at[c, s],
            recv_sem=recv2.at[c, s],
            device_id=(tm, to),
            device_id_type=MESH,
        )

    def landed1(c, s):
        source = peer(s)
        here = rx1.at[c, source]
        return pltpu.make_async_remote_copy(
            src_ref=here, dst_ref=here, send_sem=send1.at[c, s], recv_sem=recv1.at[c, s],
            device_id=(tm, source), device_id_type=MESH,
        )

    def landed2(c, s):
        source = peer(s)
        here = rx2.at[tm, c, source]
        return pltpu.make_async_remote_copy(
            src_ref=here, dst_ref=here, send_sem=send2.at[c, s], recv_sem=recv2.at[c, s],
            device_id=(tm, source), device_id_type=MESH,
        )

    def copy3(c, source, d):
        here = rx2.at[tm, c, source]
        return pltpu.make_async_remote_copy(
            src_ref=here, dst_ref=here,
            send_sem=send3.at[d, c, source], recv_sem=recv3.at[d, c, source],
            device_id=(lax.rem(tm + d, blocks), me), device_id_type=MESH,
        )

    def landed3(c, source, d):
        here = rx2.at[lax.rem(tm + blocks - d, blocks), c, source]
        return pltpu.make_async_remote_copy(
            src_ref=here, dst_ref=here,
            send_sem=send3.at[d, c, source], recv_sem=recv3.at[d, c, source],
            device_id=(lax.rem(tm + blocks - d, blocks), me), device_id_type=MESH,
        )

    def guarded(condition, act):
        if blocks == 2:
            act()
        else:
            pl.when(condition)(act)

    def needed_by(d):
        return lax.rem(tm + d, blocks) >= tm - 1

    def needed_from(d):
        return lax.rem(tm + blocks - d, blocks) <= tm + 1

    def loop(body):
        def run(i, carry):
            body(shift(i))
            return carry
        lax.fori_loop(0, parts - 1, run, 0)

    def forward(c, source):
        for d in range(1, blocks):
            guarded(needed_by(d), lambda d=d: copy3(c, source, d).start())

    for c in range(chunks):
        loop(lambda s, c=c: copy1(c, s).start())
        rx1[c, me] = pack[pl.ds(pl.multiple_of(me * blk + c * cb, TILE), cb), :]
    swap_out[...] = swap_table(angles, TILE)
    table[...] = dft_table(angles * parts, parts, unit // angles)

    for c in range(chunks):
        loop(lambda s, c=c: landed1(c, s).wait_recv())
        for q in range(per_chunk):
            field = rx1[c, :, q * unit:(q + 1) * unit, :].reshape(parts * unit, width)
            tx[c, :, q * unit:(q + 1) * unit, :] = matmul(table[...], field).reshape(parts, unit, width)
        loop(lambda s, c=c: copy2(c, s).start())
        rx2[tm, c, me] = tx[c, me]
        forward(c, me)

    span = padded // chunks

    def regroup(block, c):
        for k in range(span // TILE):
            rows_in = rx2.at[block, c].reshape(parts * cb, width)[k * step:(k + 1) * step, :]
            modes_ref[
                :, c * span + k * TILE:c * span + (k + 1) * TILE,
                pl.ds(pl.multiple_of(block * width, width), width),
            ] = matmul(swap_out[...], rows_in).reshape(angles, TILE, width)

    for c in range(chunks):
        def pass_on(s, c=c):
            landed2(c, s).wait_recv()
            forward(c, peer(s))

        for late in range(2):
            flag = parity if late == 0 else 1 - parity

            def far(j, carry, flag=flag):
                pass_on(half + 2 * j + flag)
                return carry

            def near(j, carry, flag=flag):
                s = 2 * j + 1 - flag
                pl.when(s > 0)(lambda: pass_on(s))
                return carry

            lax.fori_loop(0, half // 2, near, 0)
            lax.fori_loop(0, half // 2, far, 0)
        regroup(tm, c)

    for d in range(1, blocks):
        def take(d=d):
            for c in range(chunks):
                def arrive(i, carry, c=c):
                    landed3(c, i, d).wait_recv()
                    return carry
                lax.fori_loop(0, parts, arrive, 0)
                regroup(lax.rem(tm + blocks - d, blocks), c)

        guarded(needed_from(d), take)
        if blocks > 2:
            @pl.when(jnp.logical_not(needed_from(d)))
            def _(d=d):
                other = lax.rem(tm + blocks - d, blocks)
                modes_ref[:, :, pl.ds(pl.multiple_of(other * width, width), width)] = jnp.zeros(
                    (angles, padded, width), jnp.bfloat16
                )

    for c in range(chunks):
        loop(lambda s, c=c: copy1(c, s).wait_send())
        loop(lambda s, c=c: copy2(c, s).wait_send())
        for d in range(1, blocks):
            def sent(d=d, c=c):
                def one(i, carry):
                    copy3(c, i, d).wait_send()
                    return carry
                lax.fori_loop(0, parts, one, 0)
            guarded(needed_by(d), sent)


def gram_kernel(gain, width, modes_ref, xx_ref, xy_ref):
    tm = lax.axis_index("tm")
    count, full = modes_ref.shape[1], modes_ref.shape[3]
    limit = (tm + 1) * width
    columns = lax.broadcasted_iota(jnp.int32, (width, full), 1)
    keep_xx = columns < limit
    keep_xy = columns < jnp.minimum(limit, full - 1)
    own = pl.ds(pl.multiple_of(tm * width, width), width)
    for m in range(count):
        real, imag = modes_ref[0, m], modes_ref[1, m]
        left = jnp.concatenate([modes_ref[0, m, :, own], modes_ref[1, m, :, own]], axis=0)
        for p, right in ((0, [real, imag]), (1, [imag, -real])):
            product = lax.dot_general(
                left, jnp.concatenate(right, axis=0), (((0,), (0,)), ((), ())),
                preferred_element_type=jnp.float32,
            ) * gain
            xx_ref[m, p] = jnp.where(keep_xx, product, 0.0)
            xy_ref[m, p] = jnp.where(keep_xy, pltpu.roll(product, full - 1, 1), 0.0)


def body(parts, blocks, pressure):
    angles, rows, width = pressure.shape
    theta = angles * parts
    per_set = theta // 2 // parts
    group = max(1, TILE // angles)
    unit = group * angles
    groups = -(-rows // (parts * group))
    while parts * groups * group % TILE:
        groups += 1
    blk = unit * groups
    padded = parts * groups * group
    chunks = 1
    full = blocks * width

    vmem = pl.BlockSpec(memory_space=pltpu.VMEM)
    dma = pltpu.SemaphoreType.DMA
    modes = pl.pallas_call(
        functools.partial(exchange_kernel, parts, blocks, unit, groups, chunks),
        out_shape=jax.ShapeDtypeStruct((angles, padded, full), jnp.bfloat16),
        in_specs=[vmem],
        out_specs=vmem,
        scratch_shapes=[
            pltpu.VMEM((TILE * angles, TILE * angles), jnp.bfloat16),
            pltpu.VMEM((TILE * angles, TILE * angles), jnp.bfloat16),
            pltpu.VMEM((theta * group, theta * group), jnp.bfloat16),
            pltpu.VMEM((parts * blk, width), jnp.bfloat16),
            pltpu.VMEM((chunks, parts, blk // chunks, width), jnp.bfloat16),
            pltpu.VMEM((chunks, parts, blk // chunks, width), jnp.bfloat16),
            pltpu.VMEM((blocks, chunks, parts, blk // chunks, width), jnp.bfloat16),
            dma((chunks, parts)), dma((chunks, parts)),
            dma((chunks, parts)), dma((chunks, parts)),
            dma((blocks, chunks, parts)), dma((blocks, chunks, parts)),
        ],
        compiler_params=pltpu.CompilerParams(
            collective_id=0, has_side_effects=True, vmem_limit_bytes=48 * 2**20
        ),
        name="exchange",
    )(pressure)
    modes = modes.reshape(2, per_set, padded, full)
    shape = jax.ShapeDtypeStruct((per_set, 2, width, full), jnp.float32)
    out = pl.BlockSpec((1, 2, width, full), lambda i: (i, 0, 0, 0))
    return pl.pallas_call(
        functools.partial(gram_kernel, rows ** -0.5, width),
        grid=(per_set,),
        out_shape=(shape, shape),
        in_specs=[pl.BlockSpec((2, 1, padded, full), lambda i: (0, i, 0, 0))],
        out_specs=(out, out),
        compiler_params=pltpu.CompilerParams(vmem_limit_bytes=48 * 2**20),
        name="grams",
    )(modes)


def solution(mesh):
    parts, blocks = mesh.shape["azim"], mesh.shape["tm"]
    in_specs = (P("azim", None, "tm"),)
    out_specs = (P("azim", None, "tm", None), P("azim", None, "tm", None))
    return jax.shard_map(
        functools.partial(body, parts, blocks),
        mesh=mesh, in_specs=in_specs, out_specs=out_specs, check_vma=False,
    )
```

```python
import functools

import jax
import jax.numpy as jnp
import numpy as np
from jax import lax
from jax.experimental import pallas as pl
from jax.experimental.pallas import tpu as pltpu
from jax.sharding import PartitionSpec as P

MESH = pl.DeviceIdType.MESH
TILE = 16


def dft_table(theta, parts, group):
    angles = theta // parts
    per_set = angles // 2
    side = theta * group
    row = lax.broadcasted_iota(jnp.int32, (side, side), 0)
    column = lax.broadcasted_iota(jnp.int32, (side, side), 1)
    unit = angles * group
    within = row & (angles - 1)
    imag = (within >= per_set).astype(jnp.int32)
    wave = (row // unit) * per_set + (within & (per_set - 1))
    angle = (column // unit) * angles + (column & (angles - 1))
    index = (wave * angle + imag * (theta // 4)) & (theta - 1)
    index = jnp.where(index >= theta // 2, index - theta, index)
    values = jnp.cos(index.astype(jnp.float32) * (2.0 * np.pi / theta)) * theta ** -0.5
    if group > 1:
        same = (row & (unit - 1)) // angles == (column & (unit - 1)) // angles
        values = jnp.where(same, values, 0.0)
    return values.astype(jnp.bfloat16)


def swap_table(outer, inner):
    row = lax.broadcasted_iota(jnp.int32, (outer * inner, outer * inner), 0)
    column = lax.broadcasted_iota(jnp.int32, (outer * inner, outer * inner), 1)
    hit = (row & (inner - 1)) * outer + row // inner == column
    return jnp.where(hit, 1.0, 0.0).astype(jnp.bfloat16)


def matmul(a, pieces):
    width = pieces[0].shape[1]
    out = jnp.dot(a, jnp.concatenate(pieces, axis=1), preferred_element_type=jnp.float32)
    out = out.astype(jnp.bfloat16)
    return [out[:, i * width:(i + 1) * width] for i in range(len(pieces))]


def pairs(count):
    return [range(k, min(k + 2, count)) for k in range(0, count, 2)]


def partial_gram(left, real, imag):
    return [
        lax.dot_general(
            left, jnp.concatenate(right, axis=0), (((0,), (0,)), ((), ())),
            preferred_element_type=jnp.float32,
        )
        for right in ([real, imag], [imag, -real])
    ]


def exchange_kernel(parts, blocks, unit, groups, chunks, early, x_ref, *refs):
    if early:
        acc_ref, modes_ref, front, *refs = refs
    else:
        modes_ref, *refs = refs
    (swap_in, swap_out, table, pack, rx1, tx, rx2,
     send1, recv1, send2, recv2, send3, recv3) = refs
    me = lax.axis_index("azim")
    tm = lax.axis_index("tm")
    angles, rows, width = x_ref.shape
    blk = unit * groups
    cb = blk // chunks
    per_chunk = groups // chunks
    padded = parts * blk // angles

    barrier = pltpu.get_barrier_semaphore()

    def target(s):
        return lax.rem(me + s, parts)

    def origin(s):
        return lax.rem(me + parts - s, parts)

    def greet(s, carry):
        pl.semaphore_signal(barrier, inc=1, device_id=(tm, target(s)), device_id_type=MESH)
        return carry

    lax.fori_loop(1, parts, greet, 0)
    for d in range(1, blocks):
        pl.semaphore_signal(
            barrier, inc=1, device_id=(lax.rem(tm + d, blocks), me), device_id_type=MESH
        )

    swap_in[...] = swap_table(TILE, angles)
    step = TILE * angles
    whole = rows // TILE
    for pair in pairs(whole):
        given = [x_ref[:, k * TILE:(k + 1) * TILE, :].reshape(step, width) for k in pair]
        for k, out in zip(pair, matmul(swap_in[...], given)):
            pack[k * step:(k + 1) * step, :] = out
    for k in range(whole, padded // TILE):
        pack[k * step:(k + 1) * step, :] = jnp.zeros((step, width), jnp.bfloat16)

    pl.semaphore_wait(barrier, parts - 1 + blocks - 1)

    def shift(i):
        return 1 + lax.rem(parts // 2 - 1 + i, parts - 1)

    def copy1(c, s):
        to = target(s)
        return pltpu.make_async_remote_copy(
            src_ref=pack.at[pl.ds(pl.multiple_of(to * blk + c * cb, TILE), cb), :],
            dst_ref=rx1.at[c, me],
            send_sem=send1.at[c, s],
            recv_sem=recv1.at[c, s],
            device_id=(tm, to),
            device_id_type=MESH,
        )

    def copy2(c, s):
        to = target(s)
        return pltpu.make_async_remote_copy(
            src_ref=tx.at[c, to],
            dst_ref=rx2.at[tm, c, me],
            send_sem=send2.at[c, s],
            recv_sem=recv2.at[c, s],
            device_id=(tm, to),
            device_id_type=MESH,
        )

    def landed1(c, s):
        source = origin(s)
        here = rx1.at[c, source]
        return pltpu.make_async_remote_copy(
            src_ref=here, dst_ref=here, send_sem=send1.at[c, s], recv_sem=recv1.at[c, s],
            device_id=(tm, source), device_id_type=MESH,
        )

    def landed2(c, s):
        source = origin(s)
        here = rx2.at[tm, c, source]
        return pltpu.make_async_remote_copy(
            src_ref=here, dst_ref=here, send_sem=send2.at[c, s], recv_sem=recv2.at[c, s],
            device_id=(tm, source), device_id_type=MESH,
        )

    def copy3(c, source, d):
        here = rx2.at[tm, c, source]
        return pltpu.make_async_remote_copy(
            src_ref=here, dst_ref=here,
            send_sem=send3.at[d - 1, c, source], recv_sem=recv3.at[d - 1, c, source],
            device_id=(lax.rem(tm + d, blocks), me), device_id_type=MESH,
        )

    def landed3(c, source, d):
        here = rx2.at[lax.rem(tm + blocks - d, blocks), c, source]
        return pltpu.make_async_remote_copy(
            src_ref=here, dst_ref=here,
            send_sem=send3.at[d - 1, c, source], recv_sem=recv3.at[d - 1, c, source],
            device_id=(lax.rem(tm + blocks - d, blocks), me), device_id_type=MESH,
        )

    def guarded(condition, act):
        if blocks == 2:
            act()
        else:
            pl.when(condition)(act)

    def needed_by(d):
        return lax.rem(tm + d, blocks) >= tm - 1

    def needed_from(d):
        return lax.rem(tm + blocks - d, blocks) <= tm + 1

    def loop(body, first=0, last=parts - 1):
        def run(i, carry):
            body(shift(i))
            return carry
        lax.fori_loop(first, last, run, 0)

    def forward(c, source):
        for d in range(1, blocks):
            guarded(needed_by(d), lambda d=d: copy3(c, source, d).start())

    for c in range(chunks):
        loop(lambda s, c=c: copy1(c, s).start())
        rx1[c, me] = pack[pl.ds(pl.multiple_of(me * blk + c * cb, TILE), cb), :]
    swap_out[...] = swap_table(angles, TILE)
    table[...] = dft_table(angles * parts, parts, unit // angles)

    for c in range(chunks):
        loop(lambda s, c=c: landed1(c, s).wait_recv())
        for pair in pairs(per_chunk):
            fields = [
                rx1[c, :, q * unit:(q + 1) * unit, :].reshape(parts * unit, width) for q in pair
            ]
            for q, out in zip(pair, matmul(table[...], fields)):
                tx[c, :, q * unit:(q + 1) * unit, :] = out.reshape(parts, unit, width)
        loop(lambda s, c=c: copy2(c, s).start())
        rx2[tm, c, me] = tx[c, me]
        forward(c, me)

    span = padded // chunks

    per_set = angles // 2

    def place(block, c, k, value):
        lanes = pl.ds(pl.multiple_of(block * width, width), width)
        if c < early:
            start = c * span + k * TILE
            front[:, start:start + TILE, lanes] = value
        else:
            start = (c - early) * span + k * TILE
            modes_ref[:, start:start + TILE, lanes] = value

    def regroup(block, c):
        flat = rx2.at[block, c].reshape(parts * cb, width)
        for pair in pairs(span // TILE):
            given = [flat[k * step:(k + 1) * step, :] for k in pair]
            for k, out in zip(pair, matmul(swap_out[...], given)):
                place(block, c, k, out.reshape(angles, TILE, width))

    def take_others(c):
        for d in range(1, blocks):
            other = lax.rem(tm + blocks - d, blocks)

            def take(d=d, other=other):
                def arrive(i, carry):
                    landed3(c, i, d).wait_recv()
                    return carry
                lax.fori_loop(0, parts, arrive, 0)
                regroup(other, c)

            guarded(needed_from(d), take)
            if blocks > 2:
                @pl.when(jnp.logical_not(needed_from(d)))
                def _(other=other):
                    for k in range(span // TILE):
                        place(other, c, k, jnp.zeros((angles, TILE, width), jnp.bfloat16))

    own = pl.ds(pl.multiple_of(tm * width, width), width)

    def early_gram(m):
        left = jnp.concatenate([front[m, :, own], front[per_set + m, :, own]], axis=0)
        for p, out in enumerate(partial_gram(left, front[m], front[per_set + m])):
            acc_ref[m, p] = out

    for c in range(chunks):
        def pass_on(s, c=c):
            landed2(c, s).wait_recv()
            forward(c, origin(s))

        if early and c == chunks - 1:
            for m in range(per_set):
                early_gram(m)
                loop(pass_on, (parts - 1) * m // per_set, (parts - 1) * (m + 1) // per_set)
        else:
            loop(pass_on)
        regroup(tm, c)
        if c > 0:
            take_others(c - 1)
    take_others(chunks - 1)

    for c in range(chunks):
        loop(lambda s, c=c: copy1(c, s).wait_send())
        loop(lambda s, c=c: copy2(c, s).wait_send())
        for d in range(1, blocks):
            def sent(d=d, c=c):
                def one(i, carry):
                    copy3(c, i, d).wait_send()
                    return carry
                lax.fori_loop(0, parts, one, 0)
            guarded(needed_by(d), sent)


def gram_kernel(gain, width, has_acc, *refs):
    if has_acc:
        acc_ref, modes_ref, xx_hbm, xy_hbm, xx, xy, sem = refs
    else:
        modes_ref, xx_hbm, xy_hbm, xx, xy, sem = refs
    tm = lax.axis_index("tm")
    count, full = modes_ref.shape[0] // 2, modes_ref.shape[2]
    limit = (tm + 1) * width
    columns = lax.broadcasted_iota(jnp.int32, (width, full), 1)
    keep_xx = columns < limit
    keep_xy = columns < jnp.minimum(limit, full - 1)
    own = pl.ds(pl.multiple_of(tm * width, width), width)
    copies = []
    for m in range(count):
        left = jnp.concatenate([modes_ref[m, :, own], modes_ref[count + m, :, own]], axis=0)
        for p, product in enumerate(partial_gram(left, modes_ref[m], modes_ref[count + m])):
            if has_acc:
                product = product + acc_ref[m, p]
            product = product * gain
            xx[m, p] = jnp.where(keep_xx, product, 0.0)
            xy[m, p] = jnp.where(keep_xy, pltpu.roll(product, full - 1, 1), 0.0)
        for i, (src, dst) in enumerate(((xx, xx_hbm), (xy, xy_hbm))):
            copies.append(pltpu.make_async_copy(src.at[m], dst.at[m], sem.at[i, m]))
            copies[-1].start()
    for copy in copies:
        copy.wait()


def body(parts, blocks, pressure):
    angles, rows, width = pressure.shape
    theta = angles * parts
    per_set = theta // 2 // parts
    group = max(1, TILE // angles)
    unit = group * angles
    groups = -(-rows // (parts * group))
    while parts * groups * group % TILE:
        groups += 1
    blk = unit * groups
    padded = parts * groups * group
    chunks = max(
        c for c in range(1, 6) if groups % c == 0 and padded % (c * TILE) == 0
    )
    early = max(chunks - 2, 0)
    span = padded // chunks
    full = blocks * width

    vmem = pl.BlockSpec(memory_space=pltpu.VMEM)
    dma = pltpu.SemaphoreType.DMA
    modes_shape = jax.ShapeDtypeStruct((angles, (chunks - early) * span, full), jnp.bfloat16)
    gram_shape = jax.ShapeDtypeStruct((per_set, 2, width, full), jnp.float32)
    front = [pltpu.VMEM((angles, early * span, full), jnp.bfloat16)] if early else []
    made = pl.pallas_call(
        functools.partial(exchange_kernel, parts, blocks, unit, groups, chunks, early),
        out_shape=(gram_shape, modes_shape) if early else (modes_shape,),
        in_specs=[vmem],
        out_specs=(vmem, vmem) if early else (vmem,),
        scratch_shapes=front + [
            pltpu.VMEM((TILE * angles, TILE * angles), jnp.bfloat16),
            pltpu.VMEM((TILE * angles, TILE * angles), jnp.bfloat16),
            pltpu.VMEM((theta * group, theta * group), jnp.bfloat16),
            pltpu.VMEM((parts * blk, width), jnp.bfloat16),
            pltpu.VMEM((chunks, parts, blk // chunks, width), jnp.bfloat16),
            pltpu.VMEM((chunks, parts, blk // chunks, width), jnp.bfloat16),
            pltpu.VMEM((blocks, chunks, parts, blk // chunks, width), jnp.bfloat16),
            dma((chunks, parts)), dma((chunks, parts)),
            dma((chunks, parts)), dma((chunks, parts)),
            dma((blocks - 1, chunks, parts)), dma((blocks - 1, chunks, parts)),
        ],
        compiler_params=pltpu.CompilerParams(
            collective_id=0, has_side_effects=True, vmem_limit_bytes=48 * 2**20
        ),
        name="exchange",
    )(pressure)
    return pl.pallas_call(
        functools.partial(gram_kernel, rows ** -0.5, width, early > 0),
        out_shape=(gram_shape, gram_shape),
        in_specs=[vmem] * len(made),
        out_specs=(pl.BlockSpec(memory_space=pl.ANY),) * 2,
        scratch_shapes=[
            pltpu.VMEM(gram_shape.shape, jnp.float32),
            pltpu.VMEM(gram_shape.shape, jnp.float32),
            dma((2, per_set)),
        ],
        compiler_params=pltpu.CompilerParams(vmem_limit_bytes=48 * 2**20),
        name="grams",
    )(*made)


def solution(mesh):
    parts, blocks = mesh.shape["azim"], mesh.shape["tm"]
    in_specs = (P("azim", None, "tm"),)
    out_specs = (P("azim", None, "tm", None), P("azim", None, "tm", None))
    return jax.shard_map(
        functools.partial(body, parts, blocks),
        mesh=mesh, in_specs=in_specs, out_specs=out_specs, check_vma=False,
    )
```

```python
import functools

import jax
import jax.numpy as jnp
import numpy as np
from jax import lax
from jax.experimental import pallas as pl
from jax.experimental.pallas import tpu as pltpu
from jax.sharding import PartitionSpec as P

MESH = pl.DeviceIdType.MESH
TILE = 16


def dft_table(theta, parts, group):
    angles = theta // parts
    per_set = angles // 2
    side = theta * group
    row = lax.broadcasted_iota(jnp.int32, (side, side), 0)
    column = lax.broadcasted_iota(jnp.int32, (side, side), 1)
    unit = angles * group
    within = row & (angles - 1)
    imag = (within >= per_set).astype(jnp.int32)
    wave = (row // unit) * per_set + (within & (per_set - 1))
    angle = (column // unit) * angles + (column & (angles - 1))
    index = (wave * angle + imag * (theta // 4)) & (theta - 1)
    index = jnp.where(index >= theta // 2, index - theta, index)
    values = jnp.cos(index.astype(jnp.float32) * (2.0 * np.pi / theta)) * theta ** -0.5
    if group > 1:
        same = (row & (unit - 1)) // angles == (column & (unit - 1)) // angles
        values = jnp.where(same, values, 0.0)
    return values.astype(jnp.bfloat16)


def swap_table(outer, inner):
    row = lax.broadcasted_iota(jnp.int32, (outer * inner, outer * inner), 0)
    column = lax.broadcasted_iota(jnp.int32, (outer * inner, outer * inner), 1)
    hit = (row & (inner - 1)) * outer + row // inner == column
    return jnp.where(hit, 1.0, 0.0).astype(jnp.bfloat16)


def matmul(a, pieces):
    width = pieces[0].shape[1]
    out = jnp.dot(a, jnp.concatenate(pieces, axis=1), preferred_element_type=jnp.float32)
    out = out.astype(jnp.bfloat16)
    return [out[:, i * width:(i + 1) * width] for i in range(len(pieces))]


def pairs(count):
    return [range(k, min(k + 2, count)) for k in range(0, count, 2)]


def partial_gram(left, real, imag):
    return [
        lax.dot_general(
            left, jnp.concatenate(right, axis=0), (((0,), (0,)), ((), ())),
            preferred_element_type=jnp.float32,
        )
        for right in ([real, imag], [imag, -real])
    ]


def exchange_kernel(parts, blocks, unit, groups, chunks, early, x_ref, *refs):
    if early:
        acc_ref, modes_ref, front, *refs = refs
    else:
        modes_ref, *refs = refs
    (swap_in, swap_out, table, pack, rx1, tx, rx2,
     send1, recv1, send2, recv2, send3, recv3) = refs
    me = lax.axis_index("azim")
    tm = lax.axis_index("tm")
    angles, rows, width = x_ref.shape
    blk = unit * groups
    cb = blk // chunks
    per_chunk = groups // chunks
    padded = parts * blk // angles

    barrier = pltpu.get_barrier_semaphore()

    def target(s):
        return lax.rem(me + s, parts)

    def origin(s):
        return lax.rem(me + parts - s, parts)

    def greet(s, carry):
        pl.semaphore_signal(barrier, inc=1, device_id=(tm, target(s)), device_id_type=MESH)
        return carry

    lax.fori_loop(1, parts, greet, 0)
    for d in range(1, blocks):
        pl.semaphore_signal(
            barrier, inc=1, device_id=(lax.rem(tm + d, blocks), me), device_id_type=MESH
        )

    swap_in[...] = swap_table(TILE, angles)
    step = TILE * angles
    whole = rows // TILE
    for pair in pairs(whole):
        given = [x_ref[:, k * TILE:(k + 1) * TILE, :].reshape(step, width) for k in pair]
        for k, out in zip(pair, matmul(swap_in[...], given)):
            pack[k * step:(k + 1) * step, :] = out
    for k in range(whole, padded // TILE):
        pack[k * step:(k + 1) * step, :] = jnp.zeros((step, width), jnp.bfloat16)

    pl.semaphore_wait(barrier, parts - 1 + blocks - 1)

    def shift(i):
        return 1 + lax.rem(parts // 2 - 1 + i, parts - 1)

    def copy1(c, s):
        to = target(s)
        return pltpu.make_async_remote_copy(
            src_ref=pack.at[pl.ds(pl.multiple_of(to * blk + c * cb, TILE), cb), :],
            dst_ref=rx1.at[c, me],
            send_sem=send1.at[c, s],
            recv_sem=recv1.at[c, s],
            device_id=(tm, to),
            device_id_type=MESH,
        )

    def copy2(c, s):
        to = target(s)
        return pltpu.make_async_remote_copy(
            src_ref=tx.at[c, to],
            dst_ref=rx2.at[tm, c, me],
            send_sem=send2.at[c, s],
            recv_sem=recv2.at[c, s],
            device_id=(tm, to),
            device_id_type=MESH,
        )

    def landed1(c, s):
        source = origin(s)
        here = rx1.at[c, source]
        return pltpu.make_async_remote_copy(
            src_ref=here, dst_ref=here, send_sem=send1.at[c, s], recv_sem=recv1.at[c, s],
            device_id=(tm, source), device_id_type=MESH,
        )

    def landed2(c, s):
        source = origin(s)
        here = rx2.at[tm, c, source]
        return pltpu.make_async_remote_copy(
            src_ref=here, dst_ref=here, send_sem=send2.at[c, s], recv_sem=recv2.at[c, s],
            device_id=(tm, source), device_id_type=MESH,
        )

    def copy3(c, source, d):
        here = rx2.at[tm, c, source]
        return pltpu.make_async_remote_copy(
            src_ref=here, dst_ref=here,
            send_sem=send3.at[d - 1, c, source], recv_sem=recv3.at[d - 1, c, source],
            device_id=(lax.rem(tm + d, blocks), me), device_id_type=MESH,
        )

    def landed3(c, source, d):
        here = rx2.at[lax.rem(tm + blocks - d, blocks), c, source]
        return pltpu.make_async_remote_copy(
            src_ref=here, dst_ref=here,
            send_sem=send3.at[d - 1, c, source], recv_sem=recv3.at[d - 1, c, source],
            device_id=(lax.rem(tm + blocks - d, blocks), me), device_id_type=MESH,
        )

    def guarded(condition, act):
        if blocks == 2:
            act()
        else:
            pl.when(condition)(act)

    def needed_by(d):
        return lax.rem(tm + d, blocks) >= tm - 1

    def needed_from(d):
        return lax.rem(tm + blocks - d, blocks) <= tm + 1

    def loop(body, first=0, last=parts - 1):
        def run(i, carry):
            body(shift(i))
            return carry
        lax.fori_loop(first, last, run, 0)

    def forward(c, source):
        for d in range(1, blocks):
            guarded(needed_by(d), lambda d=d: copy3(c, source, d).start())

    for c in range(chunks):
        loop(lambda s, c=c: copy1(c, s).start())
        rx1[c, me] = pack[pl.ds(pl.multiple_of(me * blk + c * cb, TILE), cb), :]
    swap_out[...] = swap_table(angles, TILE)
    table[...] = dft_table(angles * parts, parts, unit // angles)

    for c in range(chunks):
        loop(lambda s, c=c: landed1(c, s).wait_recv())
        for pair in pairs(per_chunk):
            fields = [
                rx1[c, :, q * unit:(q + 1) * unit, :].reshape(parts * unit, width) for q in pair
            ]
            for q, out in zip(pair, matmul(table[...], fields)):
                tx[c, :, q * unit:(q + 1) * unit, :] = out.reshape(parts, unit, width)
        loop(lambda s, c=c: copy2(c, s).start())
        rx2[tm, c, me] = tx[c, me]
        forward(c, me)

    span = padded // chunks

    per_set = angles // 2

    def place(block, c, k, value):
        lanes = pl.ds(pl.multiple_of(block * width, width), width)
        if c < early:
            start = c * span + k * TILE
            front[:, start:start + TILE, lanes] = value
        else:
            start = (c - early) * span + k * TILE
            modes_ref[:, start:start + TILE, lanes] = value

    def regroup(block, c):
        flat = rx2.at[block, c].reshape(parts * cb, width)
        for pair in pairs(span // TILE):
            given = [flat[k * step:(k + 1) * step, :] for k in pair]
            for k, out in zip(pair, matmul(swap_out[...], given)):
                place(block, c, k, out.reshape(angles, TILE, width))

    def take_others(c):
        for d in range(1, blocks):
            other = lax.rem(tm + blocks - d, blocks)

            def take(d=d, other=other):
                def arrive(i, carry):
                    landed3(c, i, d).wait_recv()
                    return carry
                lax.fori_loop(0, parts, arrive, 0)
                regroup(other, c)

            guarded(needed_from(d), take)
            if blocks > 2:
                @pl.when(jnp.logical_not(needed_from(d)))
                def _(other=other):
                    for k in range(span // TILE):
                        place(other, c, k, jnp.zeros((angles, TILE, width), jnp.bfloat16))

    own = pl.ds(pl.multiple_of(tm * width, width), width)

    def early_gram(m):
        left = jnp.concatenate([front[m, :, own], front[per_set + m, :, own]], axis=0)
        for p, out in enumerate(partial_gram(left, front[m], front[per_set + m])):
            acc_ref[m, p] = out

    for c in range(chunks):
        def pass_on(s, c=c):
            landed2(c, s).wait_recv()
            forward(c, origin(s))

        if early and c == chunks - 1:
            head = parts // 4
            loop(pass_on, 0, head)
            for e in range(early):
                take_others(e)
            rest = parts - 1 - head
            for m in range(per_set):
                early_gram(m)
                loop(pass_on, head + rest * m // per_set, head + rest * (m + 1) // per_set)
        else:
            loop(pass_on)
        regroup(tm, c)
    for c in range(early, chunks):
        take_others(c)

    for c in range(chunks):
        loop(lambda s, c=c: copy1(c, s).wait_send())
        loop(lambda s, c=c: copy2(c, s).wait_send())
        for d in range(1, blocks):
            def sent(d=d, c=c):
                def one(i, carry):
                    copy3(c, i, d).wait_send()
                    return carry
                lax.fori_loop(0, parts, one, 0)
            guarded(needed_by(d), sent)


def gram_kernel(gain, width, has_acc, *refs):
    if has_acc:
        acc_ref, modes_ref, xx_hbm, xy_hbm, xx, xy, sem = refs
    else:
        modes_ref, xx_hbm, xy_hbm, xx, xy, sem = refs
    tm = lax.axis_index("tm")
    count, full = modes_ref.shape[0] // 2, modes_ref.shape[2]
    limit = (tm + 1) * width
    columns = lax.broadcasted_iota(jnp.int32, (width, full), 1)
    keep_xx = columns < limit
    keep_xy = columns < jnp.minimum(limit, full - 1)
    own = pl.ds(pl.multiple_of(tm * width, width), width)
    copies = []
    for m in range(count):
        left = jnp.concatenate([modes_ref[m, :, own], modes_ref[count + m, :, own]], axis=0)
        for p, product in enumerate(partial_gram(left, modes_ref[m], modes_ref[count + m])):
            if has_acc:
                product = product + acc_ref[m, p]
            product = product * gain
            xx[m, p] = jnp.where(keep_xx, product, 0.0)
            xy[m, p] = jnp.where(keep_xy, pltpu.roll(product, full - 1, 1), 0.0)
        for i, (src, dst) in enumerate(((xx, xx_hbm), (xy, xy_hbm))):
            copies.append(pltpu.make_async_copy(src.at[m], dst.at[m], sem.at[i, m]))
            copies[-1].start()
    for copy in copies:
        copy.wait()


def body(parts, blocks, pressure):
    angles, rows, width = pressure.shape
    theta = angles * parts
    per_set = theta // 2 // parts
    group = max(1, TILE // angles)
    unit = group * angles
    groups = -(-rows // (parts * group))
    while parts * groups * group % TILE:
        groups += 1
    blk = unit * groups
    padded = parts * groups * group
    chunks = max(
        c for c in (1, 2) if groups % c == 0 and padded % (c * TILE) == 0
    )
    early = chunks // 2
    span = padded // chunks
    full = blocks * width

    vmem = pl.BlockSpec(memory_space=pltpu.VMEM)
    dma = pltpu.SemaphoreType.DMA
    modes_shape = jax.ShapeDtypeStruct((angles, (chunks - early) * span, full), jnp.bfloat16)
    gram_shape = jax.ShapeDtypeStruct((per_set, 2, width, full), jnp.float32)
    front = [pltpu.VMEM((angles, early * span, full), jnp.bfloat16)] if early else []
    made = pl.pallas_call(
        functools.partial(exchange_kernel, parts, blocks, unit, groups, chunks, early),
        out_shape=(gram_shape, modes_shape) if early else (modes_shape,),
        in_specs=[vmem],
        out_specs=(vmem, vmem) if early else (vmem,),
        scratch_shapes=front + [
            pltpu.VMEM((TILE * angles, TILE * angles), jnp.bfloat16),
            pltpu.VMEM((TILE * angles, TILE * angles), jnp.bfloat16),
            pltpu.VMEM((theta * group, theta * group), jnp.bfloat16),
            pltpu.VMEM((parts * blk, width), jnp.bfloat16),
            pltpu.VMEM((chunks, parts, blk // chunks, width), jnp.bfloat16),
            pltpu.VMEM((chunks, parts, blk // chunks, width), jnp.bfloat16),
            pltpu.VMEM((blocks, chunks, parts, blk // chunks, width), jnp.bfloat16),
            dma((chunks, parts)), dma((chunks, parts)),
            dma((chunks, parts)), dma((chunks, parts)),
            dma((blocks - 1, chunks, parts)), dma((blocks - 1, chunks, parts)),
        ],
        compiler_params=pltpu.CompilerParams(
            collective_id=0, has_side_effects=True, vmem_limit_bytes=48 * 2**20
        ),
        name="exchange",
    )(pressure)
    return pl.pallas_call(
        functools.partial(gram_kernel, rows ** -0.5, width, early > 0),
        out_shape=(gram_shape, gram_shape),
        in_specs=[vmem] * len(made),
        out_specs=(pl.BlockSpec(memory_space=pl.ANY),) * 2,
        scratch_shapes=[
            pltpu.VMEM(gram_shape.shape, jnp.float32),
            pltpu.VMEM(gram_shape.shape, jnp.float32),
            dma((2, per_set)),
        ],
        compiler_params=pltpu.CompilerParams(vmem_limit_bytes=48 * 2**20),
        name="grams",
    )(*made)


def solution(mesh):
    parts, blocks = mesh.shape["azim"], mesh.shape["tm"]
    in_specs = (P("azim", None, "tm"),)
    out_specs = (P("azim", None, "tm", None), P("azim", None, "tm", None))
    return jax.shard_map(
        functools.partial(body, parts, blocks),
        mesh=mesh, in_specs=in_specs, out_specs=out_specs, check_vma=False,
    )
```

```python
import functools

import jax
import jax.numpy as jnp
import numpy as np
from jax import lax
from jax.experimental import pallas as pl
from jax.experimental.pallas import tpu as pltpu
from jax.sharding import PartitionSpec as P

MESH = pl.DeviceIdType.MESH
TILE = 16


def dft_table(theta, parts, group):
    angles = theta // parts
    per_set = angles // 2
    side = theta * group
    row = lax.broadcasted_iota(jnp.int32, (side, side), 0)
    column = lax.broadcasted_iota(jnp.int32, (side, side), 1)
    unit = angles * group
    within = row & (angles - 1)
    imag = (within >= per_set).astype(jnp.int32)
    wave = (row // unit) * per_set + (within & (per_set - 1))
    angle = (column // unit) * angles + (column & (angles - 1))
    index = (wave * angle + imag * (theta // 4)) & (theta - 1)
    index = jnp.where(index >= theta // 2, index - theta, index)
    values = jnp.cos(index.astype(jnp.float32) * (2.0 * np.pi / theta)) * theta ** -0.5
    if group > 1:
        same = (row & (unit - 1)) // angles == (column & (unit - 1)) // angles
        values = jnp.where(same, values, 0.0)
    return values.astype(jnp.bfloat16)


def swap_table(outer, inner):
    row = lax.broadcasted_iota(jnp.int32, (outer * inner, outer * inner), 0)
    column = lax.broadcasted_iota(jnp.int32, (outer * inner, outer * inner), 1)
    hit = (row & (inner - 1)) * outer + row // inner == column
    return jnp.where(hit, 1.0, 0.0).astype(jnp.bfloat16)


def matmul(a, pieces):
    width = pieces[0].shape[1]
    out = jnp.dot(a, jnp.concatenate(pieces, axis=1), preferred_element_type=jnp.float32)
    out = out.astype(jnp.bfloat16)
    return [out[:, i * width:(i + 1) * width] for i in range(len(pieces))]


def pairs(count):
    return [range(k, min(k + 2, count)) for k in range(0, count, 2)]


def partial_gram(left, real, imag):
    return [
        lax.dot_general(
            left, jnp.concatenate(right, axis=0), (((0,), (0,)), ((), ())),
            preferred_element_type=jnp.float32,
        )
        for right in ([real, imag], [imag, -real])
    ]


def exchange_kernel(parts, blocks, unit, groups, chunks, early, x_ref, *refs):
    if early:
        acc_ref, modes_ref, front, *refs = refs
    else:
        modes_ref, *refs = refs
    (swap_in, swap_out, table, pack, rx1, tx, rx2,
     send1, recv1, send2, recv2, send3, recv3) = refs
    me = lax.axis_index("azim")
    tm = lax.axis_index("tm")
    angles, rows, width = x_ref.shape
    blk = unit * groups
    cb = blk // chunks
    per_chunk = groups // chunks
    padded = parts * blk // angles

    barrier = pltpu.get_barrier_semaphore()

    def target(s):
        return lax.rem(me + s, parts)

    def origin(s):
        return lax.rem(me + parts - s, parts)

    def greet(s, carry):
        pl.semaphore_signal(barrier, inc=1, device_id=(tm, target(s)), device_id_type=MESH)
        return carry

    lax.fori_loop(1, parts, greet, 0)
    for d in range(1, blocks):
        pl.semaphore_signal(
            barrier, inc=1, device_id=(lax.rem(tm + d, blocks), me), device_id_type=MESH
        )

    swap_in[...] = swap_table(TILE, angles)
    step = TILE * angles
    whole = rows // TILE
    for pair in pairs(whole):
        given = [x_ref[:, k * TILE:(k + 1) * TILE, :].reshape(step, width) for k in pair]
        for k, out in zip(pair, matmul(swap_in[...], given)):
            pack[k * step:(k + 1) * step, :] = out
    for k in range(whole, padded // TILE):
        pack[k * step:(k + 1) * step, :] = jnp.zeros((step, width), jnp.bfloat16)

    pl.semaphore_wait(barrier, parts - 1 + blocks - 1)

    def order(parity, i):
        return 1 + lax.rem((1 - parity) * (parts // 2 - 1) + i, parts - 1)

    def shift(i):
        return order(lax.rem(me, 2), i)

    def copy1(c, s):
        to = target(s)
        return pltpu.make_async_remote_copy(
            src_ref=pack.at[pl.ds(pl.multiple_of(to * blk + c * cb, TILE), cb), :],
            dst_ref=rx1.at[c, me],
            send_sem=send1.at[c, s],
            recv_sem=recv1.at[c, s],
            device_id=(tm, to),
            device_id_type=MESH,
        )

    def copy2(c, s):
        to = target(s)
        return pltpu.make_async_remote_copy(
            src_ref=tx.at[c, to],
            dst_ref=rx2.at[tm, c, me],
            send_sem=send2.at[c, s],
            recv_sem=recv2.at[c, s],
            device_id=(tm, to),
            device_id_type=MESH,
        )

    def landed1(c, s):
        source = origin(s)
        here = rx1.at[c, source]
        return pltpu.make_async_remote_copy(
            src_ref=here, dst_ref=here, send_sem=send1.at[c, s], recv_sem=recv1.at[c, s],
            device_id=(tm, source), device_id_type=MESH,
        )

    def landed2(c, s):
        source = origin(s)
        here = rx2.at[tm, c, source]
        return pltpu.make_async_remote_copy(
            src_ref=here, dst_ref=here, send_sem=send2.at[c, s], recv_sem=recv2.at[c, s],
            device_id=(tm, source), device_id_type=MESH,
        )

    def copy3(c, source, d):
        here = rx2.at[tm, c, source]
        return pltpu.make_async_remote_copy(
            src_ref=here, dst_ref=here,
            send_sem=send3.at[d - 1, c, source], recv_sem=recv3.at[d - 1, c, source],
            device_id=(lax.rem(tm + d, blocks), me), device_id_type=MESH,
        )

    def landed3(c, source, d):
        here = rx2.at[lax.rem(tm + blocks - d, blocks), c, source]
        return pltpu.make_async_remote_copy(
            src_ref=here, dst_ref=here,
            send_sem=send3.at[d - 1, c, source], recv_sem=recv3.at[d - 1, c, source],
            device_id=(lax.rem(tm + blocks - d, blocks), me), device_id_type=MESH,
        )

    def guarded(condition, act):
        if blocks == 2:
            act()
        else:
            pl.when(condition)(act)

    def needed_by(d):
        return lax.rem(tm + d, blocks) >= tm - 1

    def needed_from(d):
        return lax.rem(tm + blocks - d, blocks) <= tm + 1

    def loop(body, first=0, last=parts - 1):
        def run(i, carry):
            body(shift(i))
            return carry
        lax.fori_loop(first, last, run, 0)

    def arrivals(body, first=0, last=parts - 1):
        def run(i, carry):
            for parity in range(2):
                s = order(parity, i)
                pl.when(lax.rem(origin(s), 2) == parity)(functools.partial(body, s))
            return carry
        lax.fori_loop(first, last, run, 0)

    def forward(c, source):
        for d in range(1, blocks):
            guarded(needed_by(d), lambda d=d: copy3(c, source, d).start())

    for c in range(chunks):
        loop(lambda s, c=c: copy1(c, s).start())
        rx1[c, me] = pack[pl.ds(pl.multiple_of(me * blk + c * cb, TILE), cb), :]
    swap_out[...] = swap_table(angles, TILE)
    table[...] = dft_table(angles * parts, parts, unit // angles)

    for c in range(chunks):
        loop(lambda s, c=c: landed1(c, s).wait_recv())
        for pair in pairs(per_chunk):
            fields = [
                rx1[c, :, q * unit:(q + 1) * unit, :].reshape(parts * unit, width) for q in pair
            ]
            for q, out in zip(pair, matmul(table[...], fields)):
                tx[c, :, q * unit:(q + 1) * unit, :] = out.reshape(parts, unit, width)
        loop(lambda s, c=c: copy2(c, s).start())
        rx2[tm, c, me] = tx[c, me]
        forward(c, me)

    span = padded // chunks

    per_set = angles // 2

    def place(block, c, k, value):
        lanes = pl.ds(pl.multiple_of(block * width, width), width)
        if c < early:
            start = c * span + k * TILE
            front[:, start:start + TILE, lanes] = value
        else:
            start = (c - early) * span + k * TILE
            modes_ref[:, start:start + TILE, lanes] = value

    def regroup(block, c):
        flat = rx2.at[block, c].reshape(parts * cb, width)
        for pair in pairs(span // TILE):
            given = [flat[k * step:(k + 1) * step, :] for k in pair]
            for k, out in zip(pair, matmul(swap_out[...], given)):
                place(block, c, k, out.reshape(angles, TILE, width))

    def take_others(c):
        for d in range(1, blocks):
            other = lax.rem(tm + blocks - d, blocks)

            def take(d=d, other=other):
                def arrive(i, carry):
                    landed3(c, i, d).wait_recv()
                    return carry
                lax.fori_loop(0, parts, arrive, 0)
                regroup(other, c)

            guarded(needed_from(d), take)
            if blocks > 2:
                @pl.when(jnp.logical_not(needed_from(d)))
                def _(other=other):
                    for k in range(span // TILE):
                        place(other, c, k, jnp.zeros((angles, TILE, width), jnp.bfloat16))

    own = pl.ds(pl.multiple_of(tm * width, width), width)

    def early_gram(m):
        left = jnp.concatenate([front[m, :, own], front[per_set + m, :, own]], axis=0)
        for p, out in enumerate(partial_gram(left, front[m], front[per_set + m])):
            acc_ref[m, p] = out

    for c in range(chunks):
        def pass_on(s, c=c):
            landed2(c, s).wait_recv()
            forward(c, origin(s))

        if early and c == chunks - 1:
            head = parts // 4
            arrivals(pass_on, 0, head)
            for e in range(early):
                take_others(e)
            rest = parts - 1 - head
            for m in range(per_set):
                early_gram(m)
                arrivals(pass_on, head + rest * m // per_set, head + rest * (m + 1) // per_set)
        else:
            arrivals(pass_on)
        regroup(tm, c)
    for c in range(early, chunks):
        take_others(c)

    for c in range(chunks):
        loop(lambda s, c=c: copy1(c, s).wait_send())
        loop(lambda s, c=c: copy2(c, s).wait_send())
        for d in range(1, blocks):
            def sent(d=d, c=c):
                def one(i, carry):
                    copy3(c, i, d).wait_send()
                    return carry
                lax.fori_loop(0, parts, one, 0)
            guarded(needed_by(d), sent)


def gram_kernel(gain, width, has_acc, *refs):
    if has_acc:
        acc_ref, modes_ref, xx_hbm, xy_hbm, xx, xy, sem = refs
    else:
        modes_ref, xx_hbm, xy_hbm, xx, xy, sem = refs
    tm = lax.axis_index("tm")
    count, full = modes_ref.shape[0] // 2, modes_ref.shape[2]
    limit = (tm + 1) * width
    columns = lax.broadcasted_iota(jnp.int32, (width, full), 1)
    keep_xx = columns < limit
    keep_xy = columns < jnp.minimum(limit, full - 1)
    own = pl.ds(pl.multiple_of(tm * width, width), width)
    copies = []
    for m in range(count):
        left = jnp.concatenate([modes_ref[m, :, own], modes_ref[count + m, :, own]], axis=0)
        for p, product in enumerate(partial_gram(left, modes_ref[m], modes_ref[count + m])):
            if has_acc:
                product = product + acc_ref[m, p]
            product = product * gain
            xx[m, p] = jnp.where(keep_xx, product, 0.0)
            xy[m, p] = jnp.where(keep_xy, pltpu.roll(product, full - 1, 1), 0.0)
        for i, (src, dst) in enumerate(((xx, xx_hbm), (xy, xy_hbm))):
            copies.append(pltpu.make_async_copy(src.at[m], dst.at[m], sem.at[i, m]))
            copies[-1].start()
    for copy in copies:
        copy.wait()


def body(parts, blocks, pressure):
    angles, rows, width = pressure.shape
    theta = angles * parts
    per_set = theta // 2 // parts
    group = max(1, TILE // angles)
    unit = group * angles
    groups = -(-rows // (parts * group))
    while parts * groups * group % TILE:
        groups += 1
    blk = unit * groups
    padded = parts * groups * group
    chunks = max(
        c for c in (1, 2) if groups % c == 0 and padded % (c * TILE) == 0
    )
    early = chunks // 2
    span = padded // chunks
    full = blocks * width

    vmem = pl.BlockSpec(memory_space=pltpu.VMEM)
    dma = pltpu.SemaphoreType.DMA
    modes_shape = jax.ShapeDtypeStruct((angles, (chunks - early) * span, full), jnp.bfloat16)
    gram_shape = jax.ShapeDtypeStruct((per_set, 2, width, full), jnp.float32)
    front = [pltpu.VMEM((angles, early * span, full), jnp.bfloat16)] if early else []
    made = pl.pallas_call(
        functools.partial(exchange_kernel, parts, blocks, unit, groups, chunks, early),
        out_shape=(gram_shape, modes_shape) if early else (modes_shape,),
        in_specs=[vmem],
        out_specs=(vmem, vmem) if early else (vmem,),
        scratch_shapes=front + [
            pltpu.VMEM((TILE * angles, TILE * angles), jnp.bfloat16),
            pltpu.VMEM((TILE * angles, TILE * angles), jnp.bfloat16),
            pltpu.VMEM((theta * group, theta * group), jnp.bfloat16),
            pltpu.VMEM((parts * blk, width), jnp.bfloat16),
            pltpu.VMEM((chunks, parts, blk // chunks, width), jnp.bfloat16),
            pltpu.VMEM((chunks, parts, blk // chunks, width), jnp.bfloat16),
            pltpu.VMEM((blocks, chunks, parts, blk // chunks, width), jnp.bfloat16),
            dma((chunks, parts)), dma((chunks, parts)),
            dma((chunks, parts)), dma((chunks, parts)),
            dma((blocks - 1, chunks, parts)), dma((blocks - 1, chunks, parts)),
        ],
        compiler_params=pltpu.CompilerParams(
            collective_id=0, has_side_effects=True, vmem_limit_bytes=48 * 2**20
        ),
        name="exchange",
    )(pressure)
    return pl.pallas_call(
        functools.partial(gram_kernel, rows ** -0.5, width, early > 0),
        out_shape=(gram_shape, gram_shape),
        in_specs=[vmem] * len(made),
        out_specs=(pl.BlockSpec(memory_space=pl.ANY),) * 2,
        scratch_shapes=[
            pltpu.VMEM(gram_shape.shape, jnp.float32),
            pltpu.VMEM(gram_shape.shape, jnp.float32),
            dma((2, per_set)),
        ],
        compiler_params=pltpu.CompilerParams(vmem_limit_bytes=48 * 2**20),
        name="grams",
    )(*made)


def solution(mesh):
    parts, blocks = mesh.shape["azim"], mesh.shape["tm"]
    in_specs = (P("azim", None, "tm"),)
    out_specs = (P("azim", None, "tm", None), P("azim", None, "tm", None))
    return jax.shard_map(
        functools.partial(body, parts, blocks),
        mesh=mesh, in_specs=in_specs, out_specs=out_specs, check_vma=False,
    )
```

```python
import functools

import jax
import jax.numpy as jnp
import numpy as np
from jax import lax
from jax.experimental import pallas as pl
from jax.experimental.pallas import tpu as pltpu
from jax.sharding import PartitionSpec as P

MESH = pl.DeviceIdType.MESH
TILE = 16


def dft_table(theta, parts, group):
    angles = theta // parts
    per_set = angles // 2
    side = theta * group
    row = lax.broadcasted_iota(jnp.int32, (side, side), 0)
    column = lax.broadcasted_iota(jnp.int32, (side, side), 1)
    unit = angles * group
    within = row & (angles - 1)
    imag = (within >= per_set).astype(jnp.int32)
    wave = (row // unit) * per_set + (within & (per_set - 1))
    angle = (column // unit) * angles + (column & (angles - 1))
    index = (wave * angle + imag * (theta // 4)) & (theta - 1)
    index = jnp.where(index >= theta // 2, index - theta, index)
    values = jnp.cos(index.astype(jnp.float32) * (2.0 * np.pi / theta)) * theta ** -0.5
    if group > 1:
        same = (row & (unit - 1)) // angles == (column & (unit - 1)) // angles
        values = jnp.where(same, values, 0.0)
    return values.astype(jnp.bfloat16)


def swap_table(outer, inner):
    row = lax.broadcasted_iota(jnp.int32, (outer * inner, outer * inner), 0)
    column = lax.broadcasted_iota(jnp.int32, (outer * inner, outer * inner), 1)
    hit = (row & (inner - 1)) * outer + row // inner == column
    return jnp.where(hit, 1.0, 0.0).astype(jnp.bfloat16)


def matmul(a, pieces):
    width = pieces[0].shape[1]
    out = jnp.dot(a, jnp.concatenate(pieces, axis=1), preferred_element_type=jnp.float32)
    out = out.astype(jnp.bfloat16)
    return [out[:, i * width:(i + 1) * width] for i in range(len(pieces))]


def pairs(count):
    return [range(k, min(k + 2, count)) for k in range(0, count, 2)]


def partial_gram(left, real, imag):
    return [
        lax.dot_general(
            left, jnp.concatenate(right, axis=0), (((0,), (0,)), ((), ())),
            preferred_element_type=jnp.float32,
        )
        for right in ([real, imag], [imag, -real])
    ]


def exchange_kernel(parts, blocks, unit, groups, chunks, early, x_ref, *refs):
    if early:
        acc_ref, modes_ref, front, *refs = refs
    else:
        modes_ref, *refs = refs
    (swap_in, swap_out, table, pack, rx1, tx, rx2,
     send1, recv1, send2, recv2, send3, recv3) = refs
    me = lax.axis_index("azim")
    tm = lax.axis_index("tm")
    angles, rows, width = x_ref.shape
    blk = unit * groups
    cb = blk // chunks
    per_chunk = groups // chunks
    padded = parts * blk // angles

    barrier = pltpu.get_barrier_semaphore()

    def target(s):
        return lax.rem(me + s, parts)

    def origin(s):
        return lax.rem(me + parts - s, parts)

    def greet(s, carry):
        pl.semaphore_signal(barrier, inc=1, device_id=(tm, target(s)), device_id_type=MESH)
        return carry

    lax.fori_loop(1, parts, greet, 0)
    for d in range(1, blocks):
        pl.semaphore_signal(
            barrier, inc=1, device_id=(lax.rem(tm + d, blocks), me), device_id_type=MESH
        )

    swap_in[...] = swap_table(TILE, angles)
    step = TILE * angles
    whole = rows // TILE
    for pair in pairs(whole):
        given = [x_ref[:, k * TILE:(k + 1) * TILE, :].reshape(step, width) for k in pair]
        for k, out in zip(pair, matmul(swap_in[...], given)):
            pack[k * step:(k + 1) * step, :] = out
    for k in range(whole, padded // TILE):
        pack[k * step:(k + 1) * step, :] = jnp.zeros((step, width), jnp.bfloat16)

    pl.semaphore_wait(barrier, parts - 1 + blocks - 1)

    def shift(i):
        return 1 + lax.rem(parts // 2 - 1 + i, parts - 1)

    def copy1(c, s):
        to = target(s)
        return pltpu.make_async_remote_copy(
            src_ref=pack.at[pl.ds(pl.multiple_of(to * blk + c * cb, TILE), cb), :],
            dst_ref=rx1.at[c, me],
            send_sem=send1.at[c, s],
            recv_sem=recv1.at[c, s],
            device_id=(tm, to),
            device_id_type=MESH,
        )

    def copy2(c, s):
        to = target(s)
        return pltpu.make_async_remote_copy(
            src_ref=tx.at[c, to],
            dst_ref=rx2.at[tm, c, me],
            send_sem=send2.at[c, s],
            recv_sem=recv2.at[c, s],
            device_id=(tm, to),
            device_id_type=MESH,
        )

    def landed1(c, s):
        source = origin(s)
        here = rx1.at[c, source]
        return pltpu.make_async_remote_copy(
            src_ref=here, dst_ref=here, send_sem=send1.at[c, s], recv_sem=recv1.at[c, s],
            device_id=(tm, source), device_id_type=MESH,
        )

    def landed2(c, s):
        source = origin(s)
        here = rx2.at[tm, c, source]
        return pltpu.make_async_remote_copy(
            src_ref=here, dst_ref=here, send_sem=send2.at[c, s], recv_sem=recv2.at[c, s],
            device_id=(tm, source), device_id_type=MESH,
        )

    def copy3(c, source, d):
        here = rx2.at[tm, c, source]
        return pltpu.make_async_remote_copy(
            src_ref=here, dst_ref=here,
            send_sem=send3.at[d - 1, c, source], recv_sem=recv3.at[d - 1, c, source],
            device_id=(lax.rem(tm + d, blocks), me), device_id_type=MESH,
        )

    def landed3(c, source, d):
        here = rx2.at[lax.rem(tm + blocks - d, blocks), c, source]
        return pltpu.make_async_remote_copy(
            src_ref=here, dst_ref=here,
            send_sem=send3.at[d - 1, c, source], recv_sem=recv3.at[d - 1, c, source],
            device_id=(lax.rem(tm + blocks - d, blocks), me), device_id_type=MESH,
        )

    def guarded(condition, act):
        if blocks == 2:
            act()
        else:
            pl.when(condition)(act)

    def needed_by(d):
        return lax.rem(tm + d, blocks) >= tm - 1

    def needed_from(d):
        return lax.rem(tm + blocks - d, blocks) <= tm + 1

    def loop(body, first=0, last=parts - 1):
        def run(i, carry):
            body(shift(i))
            return carry
        lax.fori_loop(first, last, run, 0)

    def forward(c, source):
        for d in range(1, blocks):
            guarded(needed_by(d), lambda d=d: copy3(c, source, d).start())

    for c in range(chunks):
        loop(lambda s, c=c: copy1(c, s).start())
        rx1[c, me] = pack[pl.ds(pl.multiple_of(me * blk + c * cb, TILE), cb), :]
    swap_out[...] = swap_table(angles, TILE)
    table[...] = dft_table(angles * parts, parts, unit // angles)

    for c in range(chunks):
        loop(lambda s, c=c: landed1(c, s).wait_recv())
        for pair in pairs(per_chunk):
            fields = [
                rx1[c, :, q * unit:(q + 1) * unit, :].reshape(parts * unit, width) for q in pair
            ]
            for q, out in zip(pair, matmul(table[...], fields)):
                tx[c, :, q * unit:(q + 1) * unit, :] = out.reshape(parts, unit, width)
        if c == 0 or not early:
            loop(lambda s, c=c: copy2(c, s).start())
        rx2[tm, c, me] = tx[c, me]
        forward(c, me)

    span = padded // chunks
    window = min(6, parts - 1)
    per_set = angles // 2

    def place(block, c, k, value):
        lanes = pl.ds(pl.multiple_of(block * width, width), width)
        if c < early:
            start = c * span + k * TILE
            front[:, start:start + TILE, lanes] = value
        else:
            start = (c - early) * span + k * TILE
            modes_ref[:, start:start + TILE, lanes] = value

    def regroup(block, c):
        flat = rx2.at[block, c].reshape(parts * cb, width)
        for pair in pairs(span // TILE):
            given = [flat[k * step:(k + 1) * step, :] for k in pair]
            for k, out in zip(pair, matmul(swap_out[...], given)):
                place(block, c, k, out.reshape(angles, TILE, width))

    def take_others(c):
        for d in range(1, blocks):
            other = lax.rem(tm + blocks - d, blocks)

            def take(d=d, other=other):
                def arrive(i, carry):
                    landed3(c, i, d).wait_recv()
                    return carry
                lax.fori_loop(0, parts, arrive, 0)
                regroup(other, c)

            guarded(needed_from(d), take)
            if blocks > 2:
                @pl.when(jnp.logical_not(needed_from(d)))
                def _(other=other):
                    for k in range(span // TILE):
                        place(other, c, k, jnp.zeros((angles, TILE, width), jnp.bfloat16))

    own = pl.ds(pl.multiple_of(tm * width, width), width)

    def early_gram(m):
        left = jnp.concatenate([front[m, :, own], front[per_set + m, :, own]], axis=0)
        for p, out in enumerate(partial_gram(left, front[m], front[per_set + m])):
            acc_ref[m, p] = out

    for c in range(chunks):
        def pass_on(s, c=c):
            landed2(c, s).wait_recv()
            forward(c, origin(s))

        def pass_and_send(first, last, ahead, c=c):
            def run(i, carry):
                pass_on(shift(i))
                copy2(chunks - 1, shift(i + ahead)).start()
                return carry
            lax.fori_loop(first, last, run, 0)

        if early and c == chunks - 1:
            paced = parts - 1 - window
            head = min(parts // 4, paced)
            pass_and_send(0, head, window)
            for e in range(early):
                take_others(e)
            rest = parts - 1 - head
            for m in range(per_set):
                early_gram(m)
                first, last = head + rest * m // per_set, head + rest * (m + 1) // per_set
                if first < paced:
                    pass_and_send(first, min(last, paced), window)
                if last > paced:
                    loop(pass_on, max(first, paced), last)
        elif early and c == chunks - 2:
            loop(pass_on, 0, parts - 1 - window)
            pass_and_send(parts - 1 - window, parts - 1, window - parts + 1)
        else:
            loop(pass_on)
        regroup(tm, c)
    for c in range(early, chunks):
        take_others(c)

    for c in range(chunks):
        loop(lambda s, c=c: copy1(c, s).wait_send())
        loop(lambda s, c=c: copy2(c, s).wait_send())
        for d in range(1, blocks):
            def sent(d=d, c=c):
                def one(i, carry):
                    copy3(c, i, d).wait_send()
                    return carry
                lax.fori_loop(0, parts, one, 0)
            guarded(needed_by(d), sent)


def gram_kernel(gain, width, has_acc, *refs):
    if has_acc:
        acc_ref, modes_ref, xx_hbm, xy_hbm, xx, xy, sem = refs
    else:
        modes_ref, xx_hbm, xy_hbm, xx, xy, sem = refs
    tm = lax.axis_index("tm")
    count, full = modes_ref.shape[0] // 2, modes_ref.shape[2]
    limit = (tm + 1) * width
    columns = lax.broadcasted_iota(jnp.int32, (width, full), 1)
    keep_xx = columns < limit
    keep_xy = columns < jnp.minimum(limit, full - 1)
    own = pl.ds(pl.multiple_of(tm * width, width), width)
    copies = []
    for m in range(count):
        left = jnp.concatenate([modes_ref[m, :, own], modes_ref[count + m, :, own]], axis=0)
        for p, product in enumerate(partial_gram(left, modes_ref[m], modes_ref[count + m])):
            if has_acc:
                product = product + acc_ref[m, p]
            product = product * gain
            xx[m, p] = jnp.where(keep_xx, product, 0.0)
            xy[m, p] = jnp.where(keep_xy, pltpu.roll(product, full - 1, 1), 0.0)
        for i, (src, dst) in enumerate(((xx, xx_hbm), (xy, xy_hbm))):
            copies.append(pltpu.make_async_copy(src.at[m], dst.at[m], sem.at[i, m]))
            copies[-1].start()
    for copy in copies:
        copy.wait()


def body(parts, blocks, pressure):
    angles, rows, width = pressure.shape
    theta = angles * parts
    per_set = theta // 2 // parts
    group = max(1, TILE // angles)
    unit = group * angles
    groups = -(-rows // (parts * group))
    while parts * groups * group % TILE:
        groups += 1
    blk = unit * groups
    padded = parts * groups * group
    chunks = max(
        c for c in (1, 2) if groups % c == 0 and padded % (c * TILE) == 0
    )
    early = chunks // 2
    span = padded // chunks
    full = blocks * width

    vmem = pl.BlockSpec(memory_space=pltpu.VMEM)
    dma = pltpu.SemaphoreType.DMA
    modes_shape = jax.ShapeDtypeStruct((angles, (chunks - early) * span, full), jnp.bfloat16)
    gram_shape = jax.ShapeDtypeStruct((per_set, 2, width, full), jnp.float32)
    front = [pltpu.VMEM((angles, early * span, full), jnp.bfloat16)] if early else []
    made = pl.pallas_call(
        functools.partial(exchange_kernel, parts, blocks, unit, groups, chunks, early),
        out_shape=(gram_shape, modes_shape) if early else (modes_shape,),
        in_specs=[vmem],
        out_specs=(vmem, vmem) if early else (vmem,),
        scratch_shapes=front + [
            pltpu.VMEM((TILE * angles, TILE * angles), jnp.bfloat16),
            pltpu.VMEM((TILE * angles, TILE * angles), jnp.bfloat16),
            pltpu.VMEM((theta * group, theta * group), jnp.bfloat16),
            pltpu.VMEM((parts * blk, width), jnp.bfloat16),
            pltpu.VMEM((chunks, parts, blk // chunks, width), jnp.bfloat16),
            pltpu.VMEM((chunks, parts, blk // chunks, width), jnp.bfloat16),
            pltpu.VMEM((blocks, chunks, parts, blk // chunks, width), jnp.bfloat16),
            dma((chunks, parts)), dma((chunks, parts)),
            dma((chunks, parts)), dma((chunks, parts)),
            dma((blocks - 1, chunks, parts)), dma((blocks - 1, chunks, parts)),
        ],
        compiler_params=pltpu.CompilerParams(
            collective_id=0, has_side_effects=True, vmem_limit_bytes=48 * 2**20
        ),
        name="exchange",
    )(pressure)
    return pl.pallas_call(
        functools.partial(gram_kernel, rows ** -0.5, width, early > 0),
        out_shape=(gram_shape, gram_shape),
        in_specs=[vmem] * len(made),
        out_specs=(pl.BlockSpec(memory_space=pl.ANY),) * 2,
        scratch_shapes=[
            pltpu.VMEM(gram_shape.shape, jnp.float32),
            pltpu.VMEM(gram_shape.shape, jnp.float32),
            dma((2, per_set)),
        ],
        compiler_params=pltpu.CompilerParams(vmem_limit_bytes=48 * 2**20),
        name="grams",
    )(*made)


def solution(mesh):
    parts, blocks = mesh.shape["azim"], mesh.shape["tm"]
    in_specs = (P("azim", None, "tm"),)
    out_specs = (P("azim", None, "tm", None), P("azim", None, "tm", None))
    return jax.shard_map(
        functools.partial(body, parts, blocks),
        mesh=mesh, in_specs=in_specs, out_specs=out_specs, check_vma=False,
    )
```

```python
import functools

import jax
import jax.numpy as jnp
import numpy as np
from jax import lax
from jax.experimental import pallas as pl
from jax.experimental.pallas import tpu as pltpu
from jax.sharding import PartitionSpec as P

MESH = pl.DeviceIdType.MESH
TILE = 16


def dft_table(theta, parts, group):
    angles = theta // parts
    per_set = angles // 2
    side = theta * group
    row = lax.broadcasted_iota(jnp.int32, (side, side), 0)
    column = lax.broadcasted_iota(jnp.int32, (side, side), 1)
    unit = angles * group
    within = row & (angles - 1)
    imag = (within >= per_set).astype(jnp.int32)
    wave = (row // unit) * per_set + (within & (per_set - 1))
    angle = (column // unit) * angles + (column & (angles - 1))
    index = (wave * angle + imag * (theta // 4)) & (theta - 1)
    index = jnp.where(index >= theta // 2, index - theta, index)
    values = jnp.cos(index.astype(jnp.float32) * (2.0 * np.pi / theta)) * theta ** -0.5
    if group > 1:
        same = (row & (unit - 1)) // angles == (column & (unit - 1)) // angles
        values = jnp.where(same, values, 0.0)
    return values.astype(jnp.bfloat16)


def swap_table(outer, inner):
    row = lax.broadcasted_iota(jnp.int32, (outer * inner, outer * inner), 0)
    column = lax.broadcasted_iota(jnp.int32, (outer * inner, outer * inner), 1)
    hit = (row & (inner - 1)) * outer + row // inner == column
    return jnp.where(hit, 1.0, 0.0).astype(jnp.bfloat16)


def matmul(a, pieces):
    width = pieces[0].shape[1]
    out = jnp.dot(a, jnp.concatenate(pieces, axis=1), preferred_element_type=jnp.float32)
    out = out.astype(jnp.bfloat16)
    return [out[:, i * width:(i + 1) * width] for i in range(len(pieces))]


def pairs(count):
    return [range(k, min(k + 2, count)) for k in range(0, count, 2)]


def partial_gram(left, real, imag):
    return [
        lax.dot_general(
            left, jnp.concatenate(right, axis=0), (((0,), (0,)), ((), ())),
            preferred_element_type=jnp.float32,
        )
        for right in ([real, imag], [imag, -real])
    ]


def exchange_kernel(parts, blocks, unit, groups, chunks, early, x_ref, *refs):
    if early:
        acc_ref, modes_ref, front, *refs = refs
    else:
        modes_ref, *refs = refs
    (swap_in, swap_out, table, pack, rx1, tx, rx2,
     send1, recv1, send2, recv2, send3, recv3) = refs
    me = lax.axis_index("azim")
    tm = lax.axis_index("tm")
    angles, rows, width = x_ref.shape
    blk = unit * groups
    cb = blk // chunks
    per_chunk = groups // chunks
    padded = parts * blk // angles

    barrier = pltpu.get_barrier_semaphore()

    def target(s):
        return lax.rem(me + s, parts)

    def origin(s):
        return lax.rem(me + parts - s, parts)

    def greet(s, carry):
        pl.semaphore_signal(barrier, inc=1, device_id=(tm, target(s)), device_id_type=MESH)
        return carry

    lax.fori_loop(1, parts, greet, 0)
    for d in range(1, blocks):
        pl.semaphore_signal(
            barrier, inc=1, device_id=(lax.rem(tm + d, blocks), me), device_id_type=MESH
        )

    swap_in[...] = swap_table(TILE, angles)
    step = TILE * angles
    whole = rows // TILE
    for pair in pairs(whole):
        given = [x_ref[:, k * TILE:(k + 1) * TILE, :].reshape(step, width) for k in pair]
        for k, out in zip(pair, matmul(swap_in[...], given)):
            pack[k * step:(k + 1) * step, :] = out
    for k in range(whole, padded // TILE):
        pack[k * step:(k + 1) * step, :] = jnp.zeros((step, width), jnp.bfloat16)

    pl.semaphore_wait(barrier, parts - 1 + blocks - 1)

    def shift(i):
        return 1 + lax.rem(parts // 2 - 1 + i, parts - 1)

    def copy1(c, s):
        to = target(s)
        return pltpu.make_async_remote_copy(
            src_ref=pack.at[pl.ds(pl.multiple_of(to * blk + c * cb, TILE), cb), :],
            dst_ref=rx1.at[c, me],
            send_sem=send1.at[c],
            recv_sem=recv1.at[c],
            device_id=(tm, to),
            device_id_type=MESH,
        )

    def copy2(c, s):
        to = target(s)
        return pltpu.make_async_remote_copy(
            src_ref=tx.at[c, to],
            dst_ref=rx2.at[tm, c, me],
            send_sem=send2.at[c],
            recv_sem=recv2.at[c, s],
            device_id=(tm, to),
            device_id_type=MESH,
        )

    def all1(c):
        there = rx1.at[c, pl.ds(0, parts - 1)]
        return pltpu.make_async_remote_copy(
            src_ref=there, dst_ref=there, send_sem=send1.at[c], recv_sem=recv1.at[c],
            device_id=(tm, target(1)), device_id_type=MESH,
        )

    def all2(c):
        there = tx.at[c, pl.ds(0, parts - 1)]
        return pltpu.make_async_remote_copy(
            src_ref=there, dst_ref=there, send_sem=send2.at[c], recv_sem=recv2.at[c, 0],
            device_id=(tm, target(1)), device_id_type=MESH,
        )

    def landed2(c, s):
        source = origin(s)
        here = rx2.at[tm, c, source]
        return pltpu.make_async_remote_copy(
            src_ref=here, dst_ref=here, send_sem=send2.at[c], recv_sem=recv2.at[c, s],
            device_id=(tm, source), device_id_type=MESH,
        )

    def copy3(c, source, d):
        here = rx2.at[tm, c, source]
        return pltpu.make_async_remote_copy(
            src_ref=here, dst_ref=here,
            send_sem=send3.at[d - 1, c], recv_sem=recv3.at[d - 1, c],
            device_id=(lax.rem(tm + d, blocks), me), device_id_type=MESH,
        )

    def all3(c, d, block):
        there = rx2.at[block, c]
        return pltpu.make_async_remote_copy(
            src_ref=there, dst_ref=there, send_sem=send3.at[d - 1, c], recv_sem=recv3.at[d - 1, c],
            device_id=(lax.rem(tm + d, blocks), me), device_id_type=MESH,
        )

    def guarded(condition, act):
        if blocks == 2:
            act()
        else:
            pl.when(condition)(act)

    def needed_by(d):
        return lax.rem(tm + d, blocks) >= tm - 1

    def needed_from(d):
        return lax.rem(tm + blocks - d, blocks) <= tm + 1

    def loop(body, first=0, last=parts - 1):
        def run(i, carry):
            body(shift(i))
            return carry
        lax.fori_loop(first, last, run, 0)

    def forward(c, source):
        for d in range(1, blocks):
            guarded(needed_by(d), lambda d=d: copy3(c, source, d).start())

    for c in range(chunks):
        loop(lambda s, c=c: copy1(c, s).start())
        rx1[c, me] = pack[pl.ds(pl.multiple_of(me * blk + c * cb, TILE), cb), :]
    swap_out[...] = swap_table(angles, TILE)
    table[...] = dft_table(angles * parts, parts, unit // angles)

    for c in range(chunks):
        all1(c).wait_recv()
        for pair in pairs(per_chunk):
            fields = [
                rx1[c, :, q * unit:(q + 1) * unit, :].reshape(parts * unit, width) for q in pair
            ]
            for q, out in zip(pair, matmul(table[...], fields)):
                tx[c, :, q * unit:(q + 1) * unit, :] = out.reshape(parts, unit, width)
        loop(lambda s, c=c: copy2(c, s).start())
        rx2[tm, c, me] = tx[c, me]
        forward(c, me)

    span = padded // chunks

    per_set = angles // 2

    def place(block, c, k, value):
        lanes = pl.ds(pl.multiple_of(block * width, width), width)
        if c < early:
            start = c * span + k * TILE
            front[:, start:start + TILE, lanes] = value
        else:
            start = (c - early) * span + k * TILE
            modes_ref[:, start:start + TILE, lanes] = value

    def regroup(block, c):
        flat = rx2.at[block, c].reshape(parts * cb, width)
        for pair in pairs(span // TILE):
            given = [flat[k * step:(k + 1) * step, :] for k in pair]
            for k, out in zip(pair, matmul(swap_out[...], given)):
                place(block, c, k, out.reshape(angles, TILE, width))

    def take_others(c):
        for d in range(1, blocks):
            other = lax.rem(tm + blocks - d, blocks)

            def take(d=d, other=other):
                all3(c, d, other).wait_recv()
                regroup(other, c)

            guarded(needed_from(d), take)
            if blocks > 2:
                @pl.when(jnp.logical_not(needed_from(d)))
                def _(other=other):
                    for k in range(span // TILE):
                        place(other, c, k, jnp.zeros((angles, TILE, width), jnp.bfloat16))

    own = pl.ds(pl.multiple_of(tm * width, width), width)

    def early_gram(m):
        left = jnp.concatenate([front[m, :, own], front[per_set + m, :, own]], axis=0)
        for p, out in enumerate(partial_gram(left, front[m], front[per_set + m])):
            acc_ref[m, p] = out

    for c in range(chunks):
        def pass_on(s, c=c):
            landed2(c, s).wait_recv()
            forward(c, origin(s))

        if early and c == chunks - 1:
            head = parts // 4
            loop(pass_on, 0, head)
            for e in range(early):
                take_others(e)
            rest = parts - 1 - head
            for m in range(per_set):
                early_gram(m)
                loop(pass_on, head + rest * m // per_set, head + rest * (m + 1) // per_set)
        else:
            loop(pass_on)
        regroup(tm, c)
    for c in range(chunks):
        all1(c).wait_send()
        all2(c).wait_send()
    for c in range(early, chunks):
        take_others(c)
    for c in range(chunks):
        for d in range(1, blocks):
            guarded(needed_by(d), lambda c=c, d=d: all3(c, d, tm).wait_send())


def gram_kernel(gain, width, has_acc, *refs):
    if has_acc:
        acc_ref, modes_ref, xx_hbm, xy_hbm, xx, xy, sem = refs
    else:
        modes_ref, xx_hbm, xy_hbm, xx, xy, sem = refs
    tm = lax.axis_index("tm")
    count, full = modes_ref.shape[0] // 2, modes_ref.shape[2]
    limit = (tm + 1) * width
    columns = lax.broadcasted_iota(jnp.int32, (width, full), 1)
    keep_xx = columns < limit
    keep_xy = columns < jnp.minimum(limit, full - 1)
    own = pl.ds(pl.multiple_of(tm * width, width), width)
    copies = []
    for m in range(count):
        left = jnp.concatenate([modes_ref[m, :, own], modes_ref[count + m, :, own]], axis=0)
        for p, product in enumerate(partial_gram(left, modes_ref[m], modes_ref[count + m])):
            if has_acc:
                product = product + acc_ref[m, p]
            product = product * gain
            xx[m, p] = jnp.where(keep_xx, product, 0.0)
            xy[m, p] = jnp.where(keep_xy, pltpu.roll(product, full - 1, 1), 0.0)
        for i, (src, dst) in enumerate(((xx, xx_hbm), (xy, xy_hbm))):
            copies.append(pltpu.make_async_copy(src.at[m], dst.at[m], sem.at[i, m]))
            copies[-1].start()
    for copy in copies:
        copy.wait()


def body(parts, blocks, pressure):
    angles, rows, width = pressure.shape
    theta = angles * parts
    per_set = theta // 2 // parts
    group = max(1, TILE // angles)
    unit = group * angles
    groups = -(-rows // (parts * group))
    while parts * groups * group % TILE:
        groups += 1
    blk = unit * groups
    padded = parts * groups * group
    chunks = max(
        c for c in (1, 2) if groups % c == 0 and padded % (c * TILE) == 0
    )
    early = chunks // 2
    span = padded // chunks
    full = blocks * width

    vmem = pl.BlockSpec(memory_space=pltpu.VMEM)
    dma = pltpu.SemaphoreType.DMA
    modes_shape = jax.ShapeDtypeStruct((angles, (chunks - early) * span, full), jnp.bfloat16)
    gram_shape = jax.ShapeDtypeStruct((per_set, 2, width, full), jnp.float32)
    front = [pltpu.VMEM((angles, early * span, full), jnp.bfloat16)] if early else []
    made = pl.pallas_call(
        functools.partial(exchange_kernel, parts, blocks, unit, groups, chunks, early),
        out_shape=(gram_shape, modes_shape) if early else (modes_shape,),
        in_specs=[vmem],
        out_specs=(vmem, vmem) if early else (vmem,),
        scratch_shapes=front + [
            pltpu.VMEM((TILE * angles, TILE * angles), jnp.bfloat16),
            pltpu.VMEM((TILE * angles, TILE * angles), jnp.bfloat16),
            pltpu.VMEM((theta * group, theta * group), jnp.bfloat16),
            pltpu.VMEM((parts * blk, width), jnp.bfloat16),
            pltpu.VMEM((chunks, parts, blk // chunks, width), jnp.bfloat16),
            pltpu.VMEM((chunks, parts, blk // chunks, width), jnp.bfloat16),
            pltpu.VMEM((blocks, chunks, parts, blk // chunks, width), jnp.bfloat16),
            dma((chunks,)), dma((chunks,)),
            dma((chunks,)), dma((chunks, parts)),
            dma((blocks - 1, chunks)), dma((blocks - 1, chunks)),
        ],
        compiler_params=pltpu.CompilerParams(
            collective_id=0, has_side_effects=True, vmem_limit_bytes=48 * 2**20
        ),
        name="exchange",
    )(pressure)
    return pl.pallas_call(
        functools.partial(gram_kernel, rows ** -0.5, width, early > 0),
        out_shape=(gram_shape, gram_shape),
        in_specs=[vmem] * len(made),
        out_specs=(pl.BlockSpec(memory_space=pl.ANY),) * 2,
        scratch_shapes=[
            pltpu.VMEM(gram_shape.shape, jnp.float32),
            pltpu.VMEM(gram_shape.shape, jnp.float32),
            dma((2, per_set)),
        ],
        compiler_params=pltpu.CompilerParams(vmem_limit_bytes=48 * 2**20),
        name="grams",
    )(*made)


def solution(mesh):
    parts, blocks = mesh.shape["azim"], mesh.shape["tm"]
    in_specs = (P("azim", None, "tm"),)
    out_specs = (P("azim", None, "tm", None), P("azim", None, "tm", None))
    return jax.shard_map(
        functools.partial(body, parts, blocks),
        mesh=mesh, in_specs=in_specs, out_specs=out_specs, check_vma=False,
    )
```

```python
import functools

import jax
import jax.numpy as jnp
import numpy as np
from jax import lax
from jax.experimental import pallas as pl
from jax.experimental.pallas import tpu as pltpu
from jax.sharding import PartitionSpec as P

MESH = pl.DeviceIdType.MESH
TILE = 16


def dft_table(theta, parts, group):
    angles = theta // parts
    per_set = angles // 2
    side = theta * group
    row = lax.broadcasted_iota(jnp.int32, (side, side), 0)
    column = lax.broadcasted_iota(jnp.int32, (side, side), 1)
    unit = angles * group
    within = row & (angles - 1)
    imag = (within >= per_set).astype(jnp.int32)
    wave = (row // unit) * per_set + (within & (per_set - 1))
    angle = (column // unit) * angles + (column & (angles - 1))
    index = (wave * angle + imag * (theta // 4)) & (theta - 1)
    index = jnp.where(index >= theta // 2, index - theta, index)
    values = jnp.cos(index.astype(jnp.float32) * (2.0 * np.pi / theta)) * theta ** -0.5
    if group > 1:
        same = (row & (unit - 1)) // angles == (column & (unit - 1)) // angles
        values = jnp.where(same, values, 0.0)
    return values.astype(jnp.bfloat16)


def swap_table(outer, inner):
    row = lax.broadcasted_iota(jnp.int32, (outer * inner, outer * inner), 0)
    column = lax.broadcasted_iota(jnp.int32, (outer * inner, outer * inner), 1)
    hit = (row & (inner - 1)) * outer + row // inner == column
    return jnp.where(hit, 1.0, 0.0).astype(jnp.bfloat16)


def matmul(a, pieces):
    width = pieces[0].shape[1]
    out = jnp.dot(a, jnp.concatenate(pieces, axis=1), preferred_element_type=jnp.float32)
    out = out.astype(jnp.bfloat16)
    return [out[:, i * width:(i + 1) * width] for i in range(len(pieces))]


def pairs(count):
    return [range(k, min(k + 2, count)) for k in range(0, count, 2)]


def partial_gram(left, real, imag):
    return [
        lax.dot_general(
            left, jnp.concatenate(right, axis=0), (((0,), (0,)), ((), ())),
            preferred_element_type=jnp.float32,
        )
        for right in ([real, imag], [imag, -real])
    ]


def exchange_kernel(parts, blocks, unit, groups, chunks, early, x_ref, *refs):
    if early:
        acc_ref, modes_ref, front, *refs = refs
    else:
        modes_ref, *refs = refs
    (swap_in, swap_out, table, pack, rx1, tx, rx2,
     send1, recv1, send2, recv2, send3, recv3) = refs
    me = lax.axis_index("azim")
    tm = lax.axis_index("tm")
    angles, rows, width = x_ref.shape
    blk = unit * groups
    cb = blk // chunks
    per_chunk = groups // chunks
    padded = parts * blk // angles

    barrier = pltpu.get_barrier_semaphore()

    def target(s):
        return lax.rem(me + s, parts)

    def origin(s):
        return lax.rem(me + parts - s, parts)

    def greet(s, carry):
        pl.semaphore_signal(barrier, inc=1, device_id=(tm, target(s)), device_id_type=MESH)
        return carry

    lax.fori_loop(1, parts, greet, 0)
    for d in range(1, blocks):
        pl.semaphore_signal(
            barrier, inc=1, device_id=(lax.rem(tm + d, blocks), me), device_id_type=MESH
        )

    swap_in[...] = swap_table(TILE, angles)
    step = TILE * angles
    whole = rows // TILE
    for pair in pairs(whole):
        given = [x_ref[:, k * TILE:(k + 1) * TILE, :].reshape(step, width) for k in pair]
        for k, out in zip(pair, matmul(swap_in[...], given)):
            pack[k * step:(k + 1) * step, :] = out
    for k in range(whole, padded // TILE):
        pack[k * step:(k + 1) * step, :] = jnp.zeros((step, width), jnp.bfloat16)

    pl.semaphore_wait(barrier, parts - 1 + blocks - 1)

    def shift(i):
        return 1 + lax.rem(parts // 2 - 1 + i, parts - 1)

    def copy1(c, s):
        to = target(s)
        return pltpu.make_async_remote_copy(
            src_ref=pack.at[pl.ds(pl.multiple_of(to * blk + c * cb, TILE), cb), :],
            dst_ref=rx1.at[c, me],
            send_sem=send1.at[c],
            recv_sem=recv1.at[c],
            device_id=(tm, to),
            device_id_type=MESH,
        )

    def copy2(c, s):
        to = target(s)
        return pltpu.make_async_remote_copy(
            src_ref=tx.at[c, to],
            dst_ref=rx2.at[tm, c, me],
            send_sem=send2.at[c],
            recv_sem=recv2.at[c, s if c == chunks - 1 else 0],
            device_id=(tm, to),
            device_id_type=MESH,
        )

    def all1(c):
        there = rx1.at[c, pl.ds(0, parts - 1)]
        return pltpu.make_async_remote_copy(
            src_ref=there, dst_ref=there, send_sem=send1.at[c], recv_sem=recv1.at[c],
            device_id=(tm, target(1)), device_id_type=MESH,
        )

    def all2(c):
        there = tx.at[c, pl.ds(0, parts - 1)]
        return pltpu.make_async_remote_copy(
            src_ref=there, dst_ref=there, send_sem=send2.at[c], recv_sem=recv2.at[c, 0],
            device_id=(tm, target(1)), device_id_type=MESH,
        )

    def landed2(c, s):
        source = origin(s)
        here = rx2.at[tm, c, source]
        return pltpu.make_async_remote_copy(
            src_ref=here, dst_ref=here, send_sem=send2.at[c], recv_sem=recv2.at[c, s],
            device_id=(tm, source), device_id_type=MESH,
        )

    def copy3(c, source, d):
        here = rx2.at[tm, c, source]
        return pltpu.make_async_remote_copy(
            src_ref=here, dst_ref=here,
            send_sem=send3.at[d - 1, c], recv_sem=recv3.at[d - 1, c],
            device_id=(lax.rem(tm + d, blocks), me), device_id_type=MESH,
        )

    def all3(c, d, block):
        there = rx2.at[block, c]
        return pltpu.make_async_remote_copy(
            src_ref=there, dst_ref=there, send_sem=send3.at[d - 1, c], recv_sem=recv3.at[d - 1, c],
            device_id=(lax.rem(tm + d, blocks), me), device_id_type=MESH,
        )

    def guarded(condition, act):
        if blocks == 2:
            act()
        else:
            pl.when(condition)(act)

    def needed_by(d):
        return lax.rem(tm + d, blocks) >= tm - 1

    def needed_from(d):
        return lax.rem(tm + blocks - d, blocks) <= tm + 1

    def loop(body, first=0, last=parts - 1):
        def run(i, carry):
            body(shift(i))
            return carry
        lax.fori_loop(first, last, run, 0)

    def forward(c, source):
        for d in range(1, blocks):
            guarded(needed_by(d), lambda d=d: copy3(c, source, d).start())

    for c in range(chunks):
        loop(lambda s, c=c: copy1(c, s).start())
        rx1[c, me] = pack[pl.ds(pl.multiple_of(me * blk + c * cb, TILE), cb), :]
    swap_out[...] = swap_table(angles, TILE)
    table[...] = dft_table(angles * parts, parts, unit // angles)

    for c in range(chunks):
        all1(c).wait_recv()
        for pair in pairs(per_chunk):
            fields = [
                rx1[c, :, q * unit:(q + 1) * unit, :].reshape(parts * unit, width) for q in pair
            ]
            for q, out in zip(pair, matmul(table[...], fields)):
                tx[c, :, q * unit:(q + 1) * unit, :] = out.reshape(parts, unit, width)
        loop(lambda s, c=c: copy2(c, s).start())
        rx2[tm, c, me] = tx[c, me]
        if c == chunks - 1:
            forward(c, me)

    span = padded // chunks

    per_set = angles // 2

    def place(block, c, k, value):
        lanes = pl.ds(pl.multiple_of(block * width, width), width)
        if c < early:
            start = c * span + k * TILE
            front[:, start:start + TILE, lanes] = value
        else:
            start = (c - early) * span + k * TILE
            modes_ref[:, start:start + TILE, lanes] = value

    def regroup(block, c):
        flat = rx2.at[block, c].reshape(parts * cb, width)
        for pair in pairs(span // TILE):
            given = [flat[k * step:(k + 1) * step, :] for k in pair]
            for k, out in zip(pair, matmul(swap_out[...], given)):
                place(block, c, k, out.reshape(angles, TILE, width))

    def take_others(c):
        for d in range(1, blocks):
            other = lax.rem(tm + blocks - d, blocks)

            def take(d=d, other=other):
                all3(c, d, other).wait_recv()
                regroup(other, c)

            guarded(needed_from(d), take)
            if blocks > 2:
                @pl.when(jnp.logical_not(needed_from(d)))
                def _(other=other):
                    for k in range(span // TILE):
                        place(other, c, k, jnp.zeros((angles, TILE, width), jnp.bfloat16))

    own = pl.ds(pl.multiple_of(tm * width, width), width)

    def early_gram(m):
        left = jnp.concatenate([front[m, :, own], front[per_set + m, :, own]], axis=0)
        for p, out in enumerate(partial_gram(left, front[m], front[per_set + m])):
            acc_ref[m, p] = out

    for c in range(chunks):
        def pass_on(s, c=c):
            landed2(c, s).wait_recv()
            forward(c, origin(s))

        if early and c == chunks - 1:
            head = parts // 4
            loop(pass_on, 0, head)
            for e in range(early):
                take_others(e)
            rest = parts - 1 - head
            for m in range(per_set):
                early_gram(m)
                loop(pass_on, head + rest * m // per_set, head + rest * (m + 1) // per_set)
        elif c == chunks - 1:
            loop(pass_on)
        else:
            all2(c).wait_recv()
            for d in range(1, blocks):
                guarded(needed_by(d), lambda c=c, d=d: all3(c, d, tm).start())
        regroup(tm, c)
    for c in range(chunks):
        all1(c).wait_send()
        all2(c).wait_send()
    for c in range(early, chunks):
        take_others(c)
    for c in range(chunks):
        for d in range(1, blocks):
            guarded(needed_by(d), lambda c=c, d=d: all3(c, d, tm).wait_send())


def gram_kernel(gain, width, has_acc, *refs):
    if has_acc:
        acc_ref, modes_ref, xx_hbm, xy_hbm, xx, xy, sem = refs
    else:
        modes_ref, xx_hbm, xy_hbm, xx, xy, sem = refs
    tm = lax.axis_index("tm")
    count, full = modes_ref.shape[0] // 2, modes_ref.shape[2]
    limit = (tm + 1) * width
    columns = lax.broadcasted_iota(jnp.int32, (width, full), 1)
    keep_xx = columns < limit
    keep_xy = columns < jnp.minimum(limit, full - 1)
    own = pl.ds(pl.multiple_of(tm * width, width), width)
    copies = []
    for m in range(count):
        left = jnp.concatenate([modes_ref[m, :, own], modes_ref[count + m, :, own]], axis=0)
        for p, product in enumerate(partial_gram(left, modes_ref[m], modes_ref[count + m])):
            if has_acc:
                product = product + acc_ref[m, p]
            product = product * gain
            xx[m, p] = jnp.where(keep_xx, product, 0.0)
            xy[m, p] = jnp.where(keep_xy, pltpu.roll(product, full - 1, 1), 0.0)
        for i, (src, dst) in enumerate(((xx, xx_hbm), (xy, xy_hbm))):
            copies.append(pltpu.make_async_copy(src.at[m], dst.at[m], sem.at[i, m]))
            copies[-1].start()
    for copy in copies:
        copy.wait()


def body(parts, blocks, pressure):
    angles, rows, width = pressure.shape
    theta = angles * parts
    per_set = theta // 2 // parts
    group = max(1, TILE // angles)
    unit = group * angles
    groups = -(-rows // (parts * group))
    while parts * groups * group % TILE:
        groups += 1
    blk = unit * groups
    padded = parts * groups * group
    chunks = max(
        c for c in (1, 2) if groups % c == 0 and padded % (c * TILE) == 0
    )
    early = chunks // 2
    span = padded // chunks
    full = blocks * width

    vmem = pl.BlockSpec(memory_space=pltpu.VMEM)
    dma = pltpu.SemaphoreType.DMA
    modes_shape = jax.ShapeDtypeStruct((angles, (chunks - early) * span, full), jnp.bfloat16)
    gram_shape = jax.ShapeDtypeStruct((per_set, 2, width, full), jnp.float32)
    front = [pltpu.VMEM((angles, early * span, full), jnp.bfloat16)] if early else []
    made = pl.pallas_call(
        functools.partial(exchange_kernel, parts, blocks, unit, groups, chunks, early),
        out_shape=(gram_shape, modes_shape) if early else (modes_shape,),
        in_specs=[vmem],
        out_specs=(vmem, vmem) if early else (vmem,),
        scratch_shapes=front + [
            pltpu.VMEM((TILE * angles, TILE * angles), jnp.bfloat16),
            pltpu.VMEM((TILE * angles, TILE * angles), jnp.bfloat16),
            pltpu.VMEM((theta * group, theta * group), jnp.bfloat16),
            pltpu.VMEM((parts * blk, width), jnp.bfloat16),
            pltpu.VMEM((chunks, parts, blk // chunks, width), jnp.bfloat16),
            pltpu.VMEM((chunks, parts, blk // chunks, width), jnp.bfloat16),
            pltpu.VMEM((blocks, chunks, parts, blk // chunks, width), jnp.bfloat16),
            dma((chunks,)), dma((chunks,)),
            dma((chunks,)), dma((chunks, parts)),
            dma((blocks - 1, chunks)), dma((blocks - 1, chunks)),
        ],
        compiler_params=pltpu.CompilerParams(
            collective_id=0, has_side_effects=True, vmem_limit_bytes=48 * 2**20
        ),
        name="exchange",
    )(pressure)
    return pl.pallas_call(
        functools.partial(gram_kernel, rows ** -0.5, width, early > 0),
        out_shape=(gram_shape, gram_shape),
        in_specs=[vmem] * len(made),
        out_specs=(pl.BlockSpec(memory_space=pl.ANY),) * 2,
        scratch_shapes=[
            pltpu.VMEM(gram_shape.shape, jnp.float32),
            pltpu.VMEM(gram_shape.shape, jnp.float32),
            dma((2, per_set)),
        ],
        compiler_params=pltpu.CompilerParams(vmem_limit_bytes=48 * 2**20),
        name="grams",
    )(*made)


def solution(mesh):
    parts, blocks = mesh.shape["azim"], mesh.shape["tm"]
    in_specs = (P("azim", None, "tm"),)
    out_specs = (P("azim", None, "tm", None), P("azim", None, "tm", None))
    return jax.shard_map(
        functools.partial(body, parts, blocks),
        mesh=mesh, in_specs=in_specs, out_specs=out_specs, check_vma=False,
    )
```
